32 devices in a mesh: lat: 16 (over z, y, x), fld: 2 (over core).
Axes of the slice: x: 2, y: 2, z: 4, core: 2. Of those that a mesh axis runs over, the one named last changes fastest.
Arguments:
- grid_fields: bfloat16 [3, 16, 32, 2, 256], P(None, 'fld', 'lat'), may hold values from -6 to 6
- legendre_basis: bfloat16 [640, 2, 32, 640], P('lat', 'fld'), may hold values from -0.75 to 0.75
- owner_list: int32 [640], replicated, may hold values from 0 to 639, as said below
- wave_speed: float32 [16], P('fld'), may hold values from 1e-06 to 0.01
Outputs:
- balanced_spectra: bfloat16 [640, 2, 3, 16, 640], P('lat', None, None, 'fld')
- balanced_grid: bfloat16 [3, 16, 32, 2, 256], P(None, 'fld', 'lat')
The draws below stay inside these ranges and needn't reach their ends.
Inputs may be any that keep to these rules, and one draw needn't show every extreme that they name: owner_list is a permutation of the 640 wavenumbers; slot d * 40 + r holds a wavenumber of r * 16 to r * 16 + 15, and for each index d of lat the slots of rounds 2 i and 2 i + 1 hold wavenumbers that add up to (4 i + 2) * 16 - 1.
All inputs are finite; a program needn't handle non-finite values.
Results may differ from the reference program's by a relative error of at most 0.0074.
Values may be sent and summed in bfloat16 or wider, within the bound.
A program may use at most 128 MiB of HBM per device.

```python
import math
import jax
import jax.numpy as jnp
from jax import lax

NM = 640
MODES = 16
HALF = 32
PPAD = 256
N_LAT = 16


def draw_owner_list(key, part):
    rounds = NM // N_LAT
    pieces = []
    for round_index in range(rounds):
        shuffled = jax.random.permutation(jax.random.fold_in(key, 17 + round_index // 2), N_LAT).astype(jnp.int32)
        if round_index % 2 == 0:
            placed = shuffled
        else:
            placed = N_LAT - 1 - shuffled
        pieces.append(round_index * N_LAT + placed)
    return jnp.stack(pieces, axis=1).reshape(-1).astype(jnp.int32)


def block_levels(key, shape, shards, least, top_value):
    def one(position, parts):
        heights = jax.random.uniform(jax.random.fold_in(jax.random.fold_in(key, 6), position), (parts,), jnp.float32, least / len(shards), top_value / len(shards))
        return jnp.repeat(jnp.exp(heights), shape[position] // parts).reshape((-1,) + (1,) * (len(shape) - position - 1))

    loudness = one(*shards[0])
    for cut in shards[1:]:
        loudness = loudness * one(*cut)
    return loudness


def gaussian(key, dims, scale, limit, split=(), kind=jnp.bfloat16):
    level = block_levels(key, dims, split, -0.22, 0.18) if split else 1.0
    values = jax.random.normal(key, dims, jnp.float32) * scale * level
    return jnp.minimum(jnp.maximum(values, -limit), limit).astype(kind)


def setup_inputs(seed: int = 0) -> dict:
    streams_of = jax.random.split(jax.random.key(seed), 5)
    grid_fields = gaussian(streams_of[0], (3, MODES, HALF, 2, PPAD), 1.0, 6.0, ((1, 2), (2, 16)))
    legendre_basis = gaussian(streams_of[1], (NM, 2, HALF, NM), (2 * HALF) ** -0.5, 0.75, ((0, 16), (1, 2)))
    owner_list = draw_owner_list(jax.random.fold_in(streams_of[4], 71), 0)
    wave_speed = jnp.clip(jnp.exp(math.log(0.01) - 9.2103404 * jax.random.uniform(streams_of[3], (MODES,), jnp.float32) ** block_levels(streams_of[3], (MODES,), ((0, 2),), -0.2, 0.2)), 9.999999974752427e-07, 0.01)
    return {"grid_fields": grid_fields, "legendre_basis": legendre_basis, "owner_list": owner_list, "wave_speed": wave_speed}


def row_table(pair_index, waves, padded, wave_count):
    points = 20 + 4 * pair_index
    highest = jnp.minimum(wave_count - 1, (points - 1) // 2)
    column = jnp.arange(padded, dtype=jnp.int32)
    phase_steps = column[:, None] * waves[None, :] % points
    angles = phase_steps.astype(jnp.float32) * (jnp.float32(2.0 * math.pi) / points.astype(jnp.float32))
    scaling = 1.0 / jnp.sqrt(points.astype(jnp.float32))
    inside = (column[:, None] < points) & (waves[None, :] <= highest)
    cosine = jnp.where(inside, jnp.cos(angles) * scaling, 0.0)
    sine_part = jnp.where(inside, -jnp.sin(angles) * scaling, 0.0)
    return jnp.stack([cosine, sine_part], axis=1).astype(jnp.bfloat16)

def balance(spectra, speeds, waves):
    totals = jnp.arange(spectra.shape[-1], dtype=jnp.int32)
    degree = totals.astype(jnp.float32)
    laplace = degree * (degree + 1.0)
    stiffness = laplace[None, :] * speeds[:, None]
    retained = 1.0 / (1.0 + stiffness)
    root_term = jnp.sqrt(stiffness)
    removed = stiffness * retained
    vorticity = spectra[:, :, 0]
    divergence = spectra[:, :, 1]
    geopotential = spectra[:, :, 2]
    rossby_part = (root_term * vorticity - geopotential) * retained
    result = jnp.stack([retained * vorticity + removed * root_term * rossby_part, retained * divergence, retained * geopotential - removed * rossby_part], axis=2)
    triangle = totals[None, :] >= waves[:, None]
    return jnp.where(triangle[:, None, None, None, :], result, 0.0)

def reference(grid_fields, legendre_basis, owner_list, wave_speed):
    padded = grid_fields.shape[4]
    wave_count = owner_list.shape[0]
    half_count = grid_fields.shape[2]
    pair_ids = jnp.arange(half_count, dtype=jnp.int32)

    def analyse_row(inputs):
        pair_index, row_values = inputs
        tables = row_table(pair_index, owner_list, padded, wave_count).astype(jnp.float32)
        return jnp.einsum('fkhj,jts->tfkhs', row_values.astype(jnp.float32), tables).astype(jnp.bfloat16)
    fourier = lax.map(analyse_row, (pair_ids, jnp.moveaxis(grid_fields, 2, 0)))
    by_slot = jnp.moveaxis(fourier, 5, 0)

    def legendre(inputs):
        row_values, tables = inputs
        return jnp.einsum('ptfkh,hpn->tfkn', row_values.astype(jnp.float32), tables.astype(jnp.float32))
    spectra = lax.map(legendre, (by_slot, legendre_basis))
    balanced = balance(spectra, wave_speed, owner_list).astype(jnp.bfloat16)

    def synthesise(inputs):
        tables, values = inputs
        return jnp.einsum('hpn,tfkn->ptfkh', tables.astype(jnp.float32), values.astype(jnp.float32)).astype(jnp.bfloat16)
    fourier_new = lax.map(synthesise, (legendre_basis, balanced))
    weights = jnp.where(owner_list == 0, 1.0, 2.0).astype(jnp.float32)

    def compose_row(inputs):
        pair_index, values = inputs
        tables = row_table(pair_index, owner_list, padded, wave_count).astype(jnp.float32)
        scaled = values.astype(jnp.float32) * weights[:, None, None, None, None]
        return jnp.einsum('stfkh,jts->fkhj', scaled, tables).astype(jnp.bfloat16)
    grid_new = lax.map(compose_row, (pair_ids, jnp.moveaxis(fourier_new, 1, 0)))
    return (balanced, jnp.moveaxis(grid_new, 0, 2))
```

```python
import functools

import jax
import jax.numpy as jnp
from jax import lax
from jax.experimental import pallas as pl
from jax.experimental.pallas import tpu as pltpu
from jax.sharding import PartitionSpec as P

MESH = pl.DeviceIdType.MESH

COS_SERIES = (
    1.0,
    -19.73920440673828,
    64.93911743164062,
    -85.45014190673828,
    60.16762924194336,
    -25.967599868774414,
    6.528658390045166,
)
SIN_SERIES = (
    6.2831854820251465,
    -41.34170150756836,
    81.60513305664062,
    -76.70301818847656,
    42.02592849731445,
    -14.899847030639648,
    3.2381374835968018,
)


def polynomial(series, argument):
    total = jnp.full_like(argument, series[-1])
    for coefficient in series[-2::-1]:
        total = total * argument + coefficient
    return total


def round_up(value, multiple):
    return -(-value // multiple) * multiple


def kernel(
    sizes,
    rows_ref,
    basis_ref,
    owner_ref,
    speed_ref,
    spectra_ref,
    grid_ref,
    table,
    basis,
    forward_out,
    forward_in,
    backward_out,
    backward_in,
    by_round,
    own_sem,
    basis_sems,
    forward_sems,
    backward_sems,
):
    (ranks, halves, slots, rounds, padded_rounds, fields, modes, pairs, wave_count) = sizes
    inner = fields * modes
    half_count = ranks * pairs
    columns = table.shape[2] // 2
    block_rows = pairs * padded_rounds
    totals = basis.shape[3]
    me = lax.axis_index("lat")
    hemisphere = lax.axis_index("fld")
    other = halves - 1 - hemisphere

    own_copy = pltpu.make_async_copy(
        basis_ref.at[pl.ds(0, rounds), 0], basis.at[hemisphere], own_sem
    )
    own_copy.start()

    barrier = pltpu.get_barrier_semaphore()

    def greet(step, carry):
        peer = lax.rem(me + step, ranks)
        pl.semaphore_signal(
            barrier, inc=1, device_id=(peer, hemisphere), device_id_type=MESH
        )
        return carry

    lax.fori_loop(1, ranks, greet, 0)
    pl.semaphore_signal(barrier, inc=1, device_id=(me, other), device_id_type=MESH)

    together = max(1, 16 // padded_rounds)
    chunk = together * padded_rounds
    row_index = lax.broadcasted_iota(jnp.int32, (chunk, columns), 0)
    column = lax.broadcasted_iota(jnp.int32, (chunk, columns), 1)
    column_f = column.astype(jnp.float32)

    def fill(step, carry):
        wave = jnp.full((chunk, columns), -1, jnp.int32)
        for part in range(together):
            for index in range(rounds):
                number = owner_ref[(step * together + part) * slots + index]
                wave = jnp.where(row_index == part * padded_rounds + index, number, wave)
        product = wave.astype(jnp.float32) * column_f
        for pair in range(pairs):
            points = 20 + 4 * (me * pairs + pair)
            highest = jnp.minimum(wave_count - 1, (points - 1) // 2)
            points_f = jnp.full((1, columns), points, jnp.int32).astype(jnp.float32)
            inverse = 1.0 / points_f
            scaling = lax.rsqrt(points_f)
            turns = jnp.floor(product * inverse + 0.5)
            angle = (product - turns * points_f) * inverse
            square = angle * angle
            inside = (column < points) & (wave <= highest) & (wave >= 0)
            scale = jnp.where(inside, scaling, 0.0)
            cosine = polynomial(COS_SERIES, square) * scale
            sine = polynomial(SIN_SERIES, square) * (angle * scale)
            where = pl.ds(pl.multiple_of(step * chunk, chunk), chunk)
            table[pair, where, 0:columns] = cosine.astype(jnp.bfloat16)
            table[pair, where, columns : 2 * columns] = (-sine).astype(jnp.bfloat16)
        return carry

    lax.fori_loop(0, ranks // together, fill, 0, unroll=2)

    blocks = []
    width = halves * inner
    for pair in range(pairs):
        values = rows_ref[pair * width : (pair + 1) * width, 0:columns]
        empty = jnp.zeros_like(values)
        both = jnp.concatenate(
            [
                jnp.concatenate([values, empty], axis=1),
                jnp.concatenate([empty, values], axis=1),
            ],
            axis=0,
        )
        found = lax.dot_general(
            table[pair], both, (((1,), (1,)), ((), ())), preferred_element_type=jnp.float32
        )
        blocks.append(found.reshape(ranks, padded_rounds, 2 * width))
    forward_out[:, :, 0 : 2 * width] = jnp.concatenate(blocks, axis=1).astype(jnp.bfloat16)

    pl.semaphore_wait(barrier, ranks)

    def send(out, into, sems):
        def one(step, carry):
            peer = lax.rem(me + step, ranks)
            pltpu.make_async_remote_copy(
                src_ref=out.at[peer],
                dst_ref=into.at[me],
                send_sem=sems.at[0],
                recv_sem=sems.at[1],
                device_id=(peer, hemisphere),
                device_id_type=MESH,
            ).start()
            return carry

        lax.fori_loop(1, ranks, one, 0)
        into[me] = out[me]

    def wait(ref, sem):
        part = ref.at[pl.ds(0, ranks - 1)]
        pltpu.make_async_copy(part, part, sem).wait()

    send(forward_out, forward_in, forward_sems)
    basis_copy = pltpu.make_async_remote_copy(
        src_ref=basis_ref.at[pl.ds(0, rounds), 0],
        dst_ref=basis.at[hemisphere],
        send_sem=basis_sems.at[0],
        recv_sem=basis_sems.at[1],
        device_id=(me, other),
        device_id_type=MESH,
    )
    basis_copy.start()

    mode_index = lax.broadcasted_iota(jnp.int32, (modes, totals), 0)
    degree_i = lax.broadcasted_iota(jnp.int32, (modes, totals), 1)
    degree = degree_i.astype(jnp.float32)
    speeds = jnp.zeros((modes, totals), jnp.float32)
    for mode in range(modes):
        speeds = jnp.where(mode_index == mode, speed_ref[mode], speeds)
    stiffness = degree * (degree + 1.0) * speeds
    retained = 1.0 / (1.0 + stiffness)
    root_term = jnp.sqrt(stiffness)
    removed = stiffness * retained

    wait(forward_in, forward_sems.at[1])
    by_round[...] = forward_in[...].astype(jnp.float32).reshape(by_round.shape)
    own_copy.wait()
    basis_copy.wait_recv()

    incoming = [
        by_round[pl.ds(index, half_count, stride=padded_rounds), :] for index in range(rounds)
    ]
    by_round[...] = jnp.zeros_like(by_round)

    for index in range(rounds):
        number = owner_ref[me * slots + index]
        turned = incoming[index].T
        spectra = jnp.zeros((2 * inner, totals), jnp.float32)
        for side in range(halves):
            coefficients = jnp.concatenate(
                [
                    turned[part * width + side * inner : part * width + (side + 1) * inner]
                    for part in range(2)
                ],
                axis=0,
            ).astype(jnp.bfloat16)
            spectra = spectra + jnp.dot(
                coefficients, basis[side, index], preferred_element_type=jnp.float32
            )
        kept = degree_i >= number
        pieces = []
        for part in range(2):
            first = part * inner
            vorticity = spectra[first : first + modes]
            divergence = spectra[first + modes : first + 2 * modes]
            geopotential = spectra[first + 2 * modes : first + 3 * modes]
            rossby_part = (root_term * vorticity - geopotential) * retained
            for value in (
                retained * vorticity + removed * root_term * rossby_part,
                retained * divergence,
                retained * geopotential - removed * rossby_part,
            ):
                pieces.append(jnp.where(kept, value, 0.0))
        balanced = jnp.concatenate(pieces, axis=0).astype(jnp.bfloat16)
        spectra_ref[index] = balanced
        weight = jnp.where(number == 0, 1.0, 2.0)
        sides = [
            lax.dot_general(
                balanced,
                basis[side, index],
                (((1,), (1,)), ((), ())),
                preferred_element_type=jnp.float32,
            )
            for side in range(halves)
        ]
        ordered = [
            sides[side][part * inner : (part + 1) * inner]
            for part in range(2)
            for side in range(halves)
        ]
        spare = by_round.shape[1] - 2 * width
        if spare:
            ordered.append(jnp.zeros((spare, half_count), jnp.float32))
        by_round[pl.ds(index, half_count, stride=padded_rounds), :] = (
            jnp.concatenate(ordered, axis=0).T * weight
        )

    backward_out[...] = by_round[...].astype(jnp.bfloat16).reshape(backward_out.shape)
    send(backward_out, backward_in, backward_sems)
    wait(backward_in, backward_sems.at[1])

    for pair in range(pairs):
        first = pair * padded_rounds
        arrived = (
            backward_in[...]
            .astype(jnp.float32)[:, first : first + padded_rounds]
            .reshape(ranks * padded_rounds, by_round.shape[1])
            .T
        )
        result = jnp.zeros((width, columns), jnp.float32)
        for part in range(2):
            result = result + jnp.dot(
                arrived[part * width : (part + 1) * width].astype(jnp.bfloat16),
                table[pair, :, part * columns : (part + 1) * columns],
                preferred_element_type=jnp.float32,
            )
        grid_ref[pair * width : (pair + 1) * width, 0:columns] = result.astype(jnp.bfloat16)
        if columns < grid_ref.shape[1]:
            grid_ref[pair * width : (pair + 1) * width, columns:] = jnp.zeros(
                (width, grid_ref.shape[1] - columns), jnp.bfloat16
            )

    basis_copy.wait_send()
    wait(forward_out, forward_sems.at[0])
    wait(backward_out, backward_sems.at[0])


def per_device(ranks, halves, grid_fields, legendre_basis, owner_list, wave_speed):
    fields, modes, pairs, hemis, padded = grid_fields.shape
    slots, _, half_count, totals = legendre_basis.shape
    wave_count = owner_list.shape[0]
    longest = 20 + 4 * (half_count - 1)
    highest = min(wave_count - 1, (longest - 1) // 2)
    rounds = min(slots, highest // ranks + 1)
    padded_rounds = round_up(rounds, 8)
    columns = min(padded, round_up(longest, 128))
    lanes = round_up(2 * hemis * fields * modes, 128)
    block_rows = pairs * padded_rounds
    sizes = (ranks, halves, slots, rounds, padded_rounds, fields, modes, pairs, wave_count)
    grid_rows = jnp.transpose(grid_fields, (2, 3, 0, 1, 4)).reshape(-1, padded)
    block = pltpu.VMEM((ranks, block_rows, lanes), jnp.bfloat16)
    spectra, rows = pl.pallas_call(
        functools.partial(kernel, sizes),
        out_shape=(
            jax.ShapeDtypeStruct((rounds, 2 * fields * modes, totals), jnp.bfloat16),
            jax.ShapeDtypeStruct(grid_rows.shape, jnp.bfloat16),
        ),
        in_specs=[
            pl.BlockSpec(memory_space=pltpu.VMEM),
            pl.BlockSpec(memory_space=pltpu.HBM),
            pl.BlockSpec(memory_space=pltpu.SMEM),
            pl.BlockSpec(memory_space=pltpu.SMEM),
        ],
        out_specs=[pl.BlockSpec(memory_space=pltpu.VMEM)] * 2,
        scratch_shapes=[
            pltpu.VMEM((pairs, ranks * padded_rounds, 2 * columns), jnp.bfloat16),
            pltpu.VMEM((hemis, rounds, half_count, totals), jnp.bfloat16),
            block,
            block,
            block,
            block,
            pltpu.VMEM((ranks * block_rows, lanes), jnp.float32),
            pltpu.SemaphoreType.DMA,
            pltpu.SemaphoreType.DMA((2,)),
            pltpu.SemaphoreType.DMA((2,)),
            pltpu.SemaphoreType.DMA((2,)),
        ],
        compiler_params=pltpu.CompilerParams(
            collective_id=0, has_side_effects=True, vmem_limit_bytes=48 * 2**20
        ),
    )(grid_rows, legendre_basis, owner_list, wave_speed)
    balanced = spectra.reshape(rounds, 2, fields, modes, totals)
    if rounds < slots:
        balanced = jnp.pad(balanced, ((0, slots - rounds),) + ((0, 0),) * 4)
    balanced_grid = jnp.transpose(
        rows.reshape(pairs, hemis, fields, modes, padded), (2, 3, 0, 1, 4)
    )
    return (balanced, balanced_grid)


def solution(mesh):
    placed = (P(None, "fld", "lat", None, None), P("lat", "fld", None, None), P(), P("fld"))
    return jax.shard_map(
        functools.partial(per_device, mesh.shape["lat"], mesh.shape["fld"]),
        mesh=mesh,
        in_specs=placed,
        out_specs=(P("lat", None, None, "fld", None), P(None, "fld", "lat", None, None)),
        check_vma=False,
    )
```

```python
import functools

import jax
import jax.numpy as jnp
from jax import lax
from jax.experimental import pallas as pl
from jax.experimental.pallas import tpu as pltpu
from jax.sharding import PartitionSpec as P

MESH = pl.DeviceIdType.MESH

COS_SERIES = (
    0.9999992251396179,
    -19.738981246948242,
    64.92865753173828,
    -85.27162170410156,
    58.79049301147461,
    -21.07110595703125,
)
SIN_SERIES = (
    6.283185005187988,
    -41.341590881347656,
    81.59994506835938,
    -76.61447143554688,
    41.3428840637207,
    -12.471243858337402,
)


def polynomial(series, argument):
    total = jnp.full_like(argument, series[-1])
    for coefficient in series[-2::-1]:
        total = total * argument + coefficient
    return total


def round_up(value, multiple):
    return -(-value // multiple) * multiple


def kernel(
    sizes,
    rows_hbm,
    basis_ref,
    owner_hbm,
    speed_hbm,
    spectra_hbm,
    grid_ref,
    table,
    basis,
    forward_out,
    forward_in,
    backward_out,
    backward_in,
    by_round,
    rows_ref,
    owner_ref,
    speed_ref,
    spectra_ref,
    own_sem,
    local_sems,
    basis_sems,
    forward_sems,
    backward_sems,
):
    (ranks, halves, slots, rounds, padded_rounds, fields, modes, pairs, wave_count) = sizes
    inner = fields * modes
    half_count = ranks * pairs
    columns = table.shape[2] // 2
    block_rows = pairs * padded_rounds
    totals = basis.shape[3]
    me = lax.axis_index("lat")
    hemisphere = lax.axis_index("fld")
    other = halves - 1 - hemisphere

    own_copy = pltpu.make_async_copy(
        basis_ref.at[pl.ds(0, rounds), 0], basis.at[hemisphere], own_sem
    )
    owner_copy = pltpu.make_async_copy(owner_hbm, owner_ref, local_sems.at[0])
    speed_copy = pltpu.make_async_copy(speed_hbm, speed_ref, local_sems.at[1])
    rows_copy = pltpu.make_async_copy(rows_hbm, rows_ref, local_sems.at[2])
    spectra_copy = pltpu.make_async_copy(spectra_ref, spectra_hbm, local_sems.at[3])
    owner_copy.start()
    speed_copy.start()
    rows_copy.start()
    own_copy.start()

    barrier = pltpu.get_barrier_semaphore()

    def greet(step, carry):
        peer = lax.rem(me + step, ranks)
        pl.semaphore_signal(
            barrier, inc=1, device_id=(peer, hemisphere), device_id_type=MESH
        )
        return carry

    lax.fori_loop(1, ranks, greet, 0)
    pl.semaphore_signal(barrier, inc=1, device_id=(me, other), device_id_type=MESH)

    together = max(1, 16 // padded_rounds)
    chunk = together * padded_rounds
    row_index = lax.broadcasted_iota(jnp.int32, (chunk, columns), 0)
    column = lax.broadcasted_iota(jnp.int32, (chunk, columns), 1)
    column_f = column.astype(jnp.float32)

    def fill(step, carry):
        wave = jnp.full((chunk, columns), -1, jnp.int32)
        for part in range(together):
            for index in range(rounds):
                number = owner_ref[(step * together + part) * slots + index]
                wave = jnp.where(row_index == part * padded_rounds + index, number, wave)
        product = wave.astype(jnp.float32) * column_f
        for pair in range(pairs):
            points = 20 + 4 * (me * pairs + pair)
            highest = jnp.minimum(wave_count - 1, (points - 1) // 2)
            points_f = jnp.full((1, columns), points, jnp.int32).astype(jnp.float32)
            inverse = 1.0 / points_f
            scaling = lax.rsqrt(points_f)
            turns = jnp.floor(product * inverse + 0.5)
            angle = (product - turns * points_f) * inverse
            square = angle * angle
            inside = (column < points) & (wave <= highest) & (wave >= 0)
            scale = jnp.where(inside, scaling, 0.0)
            cosine = polynomial(COS_SERIES, square) * scale
            sine = polynomial(SIN_SERIES, square) * (angle * scale)
            where = pl.ds(pl.multiple_of(step * chunk, chunk), chunk)
            table[pair, where, 0:columns] = cosine.astype(jnp.bfloat16)
            table[pair, where, columns : 2 * columns] = (-sine).astype(jnp.bfloat16)
        return carry

    owner_copy.wait()
    lax.fori_loop(0, ranks // together, fill, 0, unroll=2)
    rows_copy.wait()

    blocks = []
    width = halves * inner
    for pair in range(pairs):
        values = rows_ref[pair * width : (pair + 1) * width, 0:columns]
        empty = jnp.zeros_like(values)
        both = jnp.concatenate(
            [
                jnp.concatenate([values, empty], axis=1),
                jnp.concatenate([empty, values], axis=1),
            ],
            axis=0,
        )
        found = lax.dot_general(
            table[pair], both, (((1,), (1,)), ((), ())), preferred_element_type=jnp.float32
        )
        blocks.append(found.reshape(ranks, padded_rounds, 2 * width))
    forward_out[:, :, 0 : 2 * width] = jnp.concatenate(blocks, axis=1).astype(jnp.bfloat16)

    pl.semaphore_wait(barrier, ranks)

    def send(out, into, sems):
        def one(step, carry):
            peer = lax.rem(me + step, ranks)
            pltpu.make_async_remote_copy(
                src_ref=out.at[peer],
                dst_ref=into.at[me],
                send_sem=sems.at[0],
                recv_sem=sems.at[1],
                device_id=(peer, hemisphere),
                device_id_type=MESH,
            ).start()
            return carry

        lax.fori_loop(1, ranks, one, 0)
        into[me] = out[me]

    def wait(ref, sem):
        part = ref.at[pl.ds(0, ranks - 1)]
        pltpu.make_async_copy(part, part, sem).wait()

    send(forward_out, forward_in, forward_sems)
    basis_copy = pltpu.make_async_remote_copy(
        src_ref=basis_ref.at[pl.ds(0, rounds), 0],
        dst_ref=basis.at[hemisphere],
        send_sem=basis_sems.at[0],
        recv_sem=basis_sems.at[1],
        device_id=(me, other),
        device_id_type=MESH,
    )
    basis_copy.start()

    speed_copy.wait()
    mode_index = lax.broadcasted_iota(jnp.int32, (modes, totals), 0)
    degree_i = lax.broadcasted_iota(jnp.int32, (modes, totals), 1)
    degree = degree_i.astype(jnp.float32)
    speeds = jnp.zeros((modes, totals), jnp.float32)
    for mode in range(modes):
        speeds = jnp.where(mode_index == mode, speed_ref[mode], speeds)
    stiffness = degree * (degree + 1.0) * speeds
    retained = 1.0 / (1.0 + stiffness)
    root_term = jnp.sqrt(stiffness)
    removed = stiffness * retained

    wait(forward_in, forward_sems.at[1])
    by_round[...] = forward_in[...].astype(jnp.float32).reshape(by_round.shape)
    own_copy.wait()
    basis_copy.wait_recv()

    incoming = [
        by_round[pl.ds(index, half_count, stride=padded_rounds), :] for index in range(rounds)
    ]
    by_round[...] = jnp.zeros_like(by_round)

    for index in range(rounds):
        number = owner_ref[me * slots + index]
        turned = incoming[index].T
        spectra = jnp.zeros((2 * inner, totals), jnp.float32)
        for side in range(halves):
            coefficients = jnp.concatenate(
                [
                    turned[part * width + side * inner : part * width + (side + 1) * inner]
                    for part in range(2)
                ],
                axis=0,
            ).astype(jnp.bfloat16)
            spectra = spectra + jnp.dot(
                coefficients, basis[side, index], preferred_element_type=jnp.float32
            )
        kept = degree_i >= number
        pieces = []
        for part in range(2):
            first = part * inner
            vorticity = spectra[first : first + modes]
            divergence = spectra[first + modes : first + 2 * modes]
            geopotential = spectra[first + 2 * modes : first + 3 * modes]
            rossby_part = (root_term * vorticity - geopotential) * retained
            for value in (
                retained * vorticity + removed * root_term * rossby_part,
                retained * divergence,
                retained * geopotential - removed * rossby_part,
            ):
                pieces.append(jnp.where(kept, value, 0.0))
        balanced = jnp.concatenate(pieces, axis=0).astype(jnp.bfloat16)
        spectra_ref[index] = balanced
        weight = jnp.where(number == 0, 1.0, 2.0)
        sides = [
            lax.dot_general(
                balanced,
                basis[side, index],
                (((1,), (1,)), ((), ())),
                preferred_element_type=jnp.float32,
            )
            for side in range(halves)
        ]
        ordered = [
            sides[side][part * inner : (part + 1) * inner]
            for part in range(2)
            for side in range(halves)
        ]
        spare = by_round.shape[1] - 2 * width
        if spare:
            ordered.append(jnp.zeros((spare, half_count), jnp.float32))
        by_round[pl.ds(index, half_count, stride=padded_rounds), :] = (
            jnp.concatenate(ordered, axis=0).T * weight
        )

    backward_out[...] = by_round[...].astype(jnp.bfloat16).reshape(backward_out.shape)
    send(backward_out, backward_in, backward_sems)
    spectra_copy.start()
    wait(backward_in, backward_sems.at[1])

    for pair in range(pairs):
        first = pair * padded_rounds
        arrived = (
            backward_in[...]
            .astype(jnp.float32)[:, first : first + padded_rounds]
            .reshape(ranks * padded_rounds, by_round.shape[1])
            .T
        )
        result = jnp.zeros((width, columns), jnp.float32)
        for part in range(2):
            result = result + jnp.dot(
                arrived[part * width : (part + 1) * width].astype(jnp.bfloat16),
                table[pair, :, part * columns : (part + 1) * columns],
                preferred_element_type=jnp.float32,
            )
        grid_ref[pair * width : (pair + 1) * width, 0:columns] = result.astype(jnp.bfloat16)
        if columns < grid_ref.shape[1]:
            grid_ref[pair * width : (pair + 1) * width, columns:] = jnp.zeros(
                (width, grid_ref.shape[1] - columns), jnp.bfloat16
            )

    spectra_copy.wait()
    basis_copy.wait_send()
    wait(forward_out, forward_sems.at[0])
    wait(backward_out, backward_sems.at[0])


def per_device(ranks, halves, grid_fields, legendre_basis, owner_list, wave_speed):
    fields, modes, pairs, hemis, padded = grid_fields.shape
    slots, _, half_count, totals = legendre_basis.shape
    wave_count = owner_list.shape[0]
    longest = 20 + 4 * (half_count - 1)
    highest = min(wave_count - 1, (longest - 1) // 2)
    rounds = min(slots, highest // ranks + 1)
    padded_rounds = round_up(rounds, 8)
    columns = min(padded, round_up(longest, 128))
    lanes = round_up(2 * hemis * fields * modes, 128)
    block_rows = pairs * padded_rounds
    sizes = (ranks, halves, slots, rounds, padded_rounds, fields, modes, pairs, wave_count)
    grid_rows = jnp.transpose(grid_fields, (2, 3, 0, 1, 4)).reshape(-1, padded)
    block = pltpu.VMEM((ranks, block_rows, lanes), jnp.bfloat16)
    spectra, rows = pl.pallas_call(
        functools.partial(kernel, sizes),
        out_shape=(
            jax.ShapeDtypeStruct((rounds, 2 * fields * modes, totals), jnp.bfloat16),
            jax.ShapeDtypeStruct(grid_rows.shape, jnp.bfloat16),
        ),
        in_specs=[pl.BlockSpec(memory_space=pltpu.HBM)] * 4,
        out_specs=[
            pl.BlockSpec(memory_space=pltpu.HBM),
            pl.BlockSpec(memory_space=pltpu.VMEM),
        ],
        scratch_shapes=[
            pltpu.VMEM((pairs, ranks * padded_rounds, 2 * columns), jnp.bfloat16),
            pltpu.VMEM((hemis, rounds, half_count, totals), jnp.bfloat16),
            block,
            block,
            block,
            block,
            pltpu.VMEM((ranks * block_rows, lanes), jnp.float32),
            pltpu.VMEM(grid_rows.shape, jnp.bfloat16),
            pltpu.SMEM(owner_list.shape, jnp.int32),
            pltpu.SMEM(wave_speed.shape, jnp.float32),
            pltpu.VMEM((rounds, 2 * fields * modes, totals), jnp.bfloat16),
            pltpu.SemaphoreType.DMA,
            pltpu.SemaphoreType.DMA((4,)),
            pltpu.SemaphoreType.DMA((2,)),
            pltpu.SemaphoreType.DMA((2,)),
            pltpu.SemaphoreType.DMA((2,)),
        ],
        compiler_params=pltpu.CompilerParams(
            collective_id=0, has_side_effects=True, vmem_limit_bytes=63 * 2**20
        ),
    )(grid_rows, legendre_basis, owner_list, wave_speed)
    balanced = spectra.reshape(rounds, 2, fields, modes, totals)
    if rounds < slots:
        balanced = jnp.pad(balanced, ((0, slots - rounds),) + ((0, 0),) * 4)
    balanced_grid = jnp.transpose(
        rows.reshape(pairs, hemis, fields, modes, padded), (2, 3, 0, 1, 4)
    )
    return (balanced, balanced_grid)


def solution(mesh):
    placed = (P(None, "fld", "lat", None, None), P("lat", "fld", None, None), P(), P("fld"))
    return jax.shard_map(
        functools.partial(per_device, mesh.shape["lat"], mesh.shape["fld"]),
        mesh=mesh,
        in_specs=placed,
        out_specs=(P("lat", None, None, "fld", None), P(None, "fld", "lat", None, None)),
        check_vma=False,
    )
```

```python
import functools

import jax
import jax.numpy as jnp
from jax import lax
from jax.experimental import pallas as pl
from jax.experimental.pallas import tpu as pltpu
from jax.sharding import PartitionSpec as P

MESH = pl.DeviceIdType.MESH

COS_SERIES = (
    0.9999992251396179,
    -19.738981246948242,
    64.92865753173828,
    -85.27162170410156,
    58.79049301147461,
    -21.07110595703125,
)
SIN_SERIES = (
    6.283185005187988,
    -41.341590881347656,
    81.59994506835938,
    -76.61447143554688,
    41.3428840637207,
    -12.471243858337402,
)


def polynomial(series, argument):
    total = jnp.full_like(argument, series[-1])
    for coefficient in series[-2::-1]:
        total = total * argument + coefficient
    return total


def round_up(value, multiple):
    return -(-value // multiple) * multiple


def kernel(
    sizes,
    rows_ref,
    basis_ref,
    owner_hbm,
    speed_hbm,
    spectra_ref,
    grid_ref,
    table,
    basis,
    forward_out,
    forward_in,
    backward_out,
    backward_in,
    by_round,
    owner_ref,
    speed_ref,
    own_sem,
    local_sems,
    basis_sems,
    forward_sems,
    backward_sems,
):
    (ranks, halves, slots, rounds, padded_rounds, fields, modes, pairs, wave_count) = sizes
    inner = fields * modes
    half_count = ranks * pairs
    columns = table.shape[2] // 2
    block_rows = pairs * padded_rounds
    totals = basis.shape[3]
    me = lax.axis_index("lat")
    hemisphere = lax.axis_index("fld")
    other = halves - 1 - hemisphere

    own_copy = pltpu.make_async_copy(
        basis_ref.at[pl.ds(0, rounds), 0], basis.at[hemisphere], own_sem
    )
    owner_copy = pltpu.make_async_copy(owner_hbm, owner_ref, local_sems.at[0])
    speed_copy = pltpu.make_async_copy(speed_hbm, speed_ref, local_sems.at[1])
    owner_copy.start()
    speed_copy.start()
    own_copy.start()

    barrier = pltpu.get_barrier_semaphore()

    def greet(step, carry):
        peer = lax.rem(me + step, ranks)
        pl.semaphore_signal(
            barrier, inc=1, device_id=(peer, hemisphere), device_id_type=MESH
        )
        return carry

    lax.fori_loop(1, ranks, greet, 0)
    pl.semaphore_signal(barrier, inc=1, device_id=(me, other), device_id_type=MESH)

    together = max(1, 16 // padded_rounds)
    chunk = together * padded_rounds
    row_index = lax.broadcasted_iota(jnp.int32, (chunk, columns), 0)
    column = lax.broadcasted_iota(jnp.int32, (chunk, columns), 1)
    column_f = column.astype(jnp.float32)

    def fill(step, carry):
        wave = jnp.full((chunk, columns), -1, jnp.int32)
        for part in range(together):
            for index in range(rounds):
                number = owner_ref[(step * together + part) * slots + index]
                wave = jnp.where(row_index == part * padded_rounds + index, number, wave)
        product = wave.astype(jnp.float32) * column_f
        for pair in range(pairs):
            points = 20 + 4 * (me * pairs + pair)
            highest = jnp.minimum(wave_count - 1, (points - 1) // 2)
            points_f = jnp.full((1, columns), points, jnp.int32).astype(jnp.float32)
            inverse = 1.0 / points_f
            scaling = lax.rsqrt(points_f)
            turns = jnp.floor(product * inverse + 0.5)
            angle = (product - turns * points_f) * inverse
            square = angle * angle
            inside = (column < points) & (wave <= highest) & (wave >= 0)
            scale = jnp.where(inside, scaling, 0.0)
            cosine = polynomial(COS_SERIES, square) * scale
            sine = polynomial(SIN_SERIES, square) * (angle * scale)
            where = pl.ds(pl.multiple_of(step * chunk, chunk), chunk)
            table[pair, where, 0:columns] = cosine.astype(jnp.bfloat16)
            table[pair, where, columns : 2 * columns] = (-sine).astype(jnp.bfloat16)
        return carry

    owner_copy.wait()
    lax.fori_loop(0, ranks // together, fill, 0, unroll=2)

    blocks = []
    width = halves * inner
    for pair in range(pairs):
        values = rows_ref[pair * width : (pair + 1) * width, 0:columns]
        empty = jnp.zeros_like(values)
        both = jnp.concatenate(
            [
                jnp.concatenate([values, empty], axis=1),
                jnp.concatenate([empty, values], axis=1),
            ],
            axis=0,
        )
        found = lax.dot_general(
            table[pair], both, (((1,), (1,)), ((), ())), preferred_element_type=jnp.float32
        )
        blocks.append(found.reshape(ranks, padded_rounds, 2 * width))
    forward_out[:, :, 0 : 2 * width] = jnp.concatenate(blocks, axis=1).astype(jnp.bfloat16)

    pl.semaphore_wait(barrier, ranks)

    def send(out, into, sems):
        def one(step, carry):
            peer = lax.rem(me + step, ranks)
            pltpu.make_async_remote_copy(
                src_ref=out.at[peer],
                dst_ref=into.at[me],
                send_sem=sems.at[0],
                recv_sem=sems.at[1],
                device_id=(peer, hemisphere),
                device_id_type=MESH,
            ).start()
            return carry

        lax.fori_loop(1, ranks, one, 0)
        into[me] = out[me]

    def wait(ref, sem):
        part = ref.at[pl.ds(0, ranks - 1)]
        pltpu.make_async_copy(part, part, sem).wait()

    send(forward_out, forward_in, forward_sems)
    basis_copy = pltpu.make_async_remote_copy(
        src_ref=basis_ref.at[pl.ds(0, rounds), 0],
        dst_ref=basis.at[hemisphere],
        send_sem=basis_sems.at[0],
        recv_sem=basis_sems.at[1],
        device_id=(me, other),
        device_id_type=MESH,
    )
    basis_copy.start()

    speed_copy.wait()
    mode_index = lax.broadcasted_iota(jnp.int32, (modes, totals), 0)
    degree_i = lax.broadcasted_iota(jnp.int32, (modes, totals), 1)
    degree = degree_i.astype(jnp.float32)
    speeds = jnp.zeros((modes, totals), jnp.float32)
    for mode in range(modes):
        speeds = jnp.where(mode_index == mode, speed_ref[mode], speeds)
    stiffness = degree * (degree + 1.0) * speeds
    retained = 1.0 / (1.0 + stiffness)
    root_term = jnp.sqrt(stiffness)
    removed = stiffness * retained

    wait(forward_in, forward_sems.at[1])
    by_round[...] = forward_in[...].astype(jnp.float32).reshape(by_round.shape)
    own_copy.wait()
    basis_copy.wait_recv()

    incoming = [
        by_round[pl.ds(index, half_count, stride=padded_rounds), :] for index in range(rounds)
    ]
    by_round[...] = jnp.zeros_like(by_round)

    for index in range(rounds):
        number = owner_ref[me * slots + index]
        turned = incoming[index].T
        spectra = jnp.zeros((2 * inner, totals), jnp.float32)
        for side in range(halves):
            coefficients = jnp.concatenate(
                [
                    turned[part * width + side * inner : part * width + (side + 1) * inner]
                    for part in range(2)
                ],
                axis=0,
            ).astype(jnp.bfloat16)
            spectra = spectra + jnp.dot(
                coefficients, basis[side, index], preferred_element_type=jnp.float32
            )
        kept = degree_i >= number
        pieces = []
        for part in range(2):
            first = part * inner
            vorticity = spectra[first : first + modes]
            divergence = spectra[first + modes : first + 2 * modes]
            geopotential = spectra[first + 2 * modes : first + 3 * modes]
            rossby_part = (root_term * vorticity - geopotential) * retained
            for value in (
                retained * vorticity + removed * root_term * rossby_part,
                retained * divergence,
                retained * geopotential - removed * rossby_part,
            ):
                pieces.append(jnp.where(kept, value, 0.0))
        balanced = jnp.concatenate(pieces, axis=0).astype(jnp.bfloat16)
        spectra_ref[index] = balanced
        weight = jnp.where(number == 0, 1.0, 2.0)
        sides = [
            lax.dot_general(
                balanced,
                basis[side, index],
                (((1,), (1,)), ((), ())),
                preferred_element_type=jnp.float32,
            )
            for side in range(halves)
        ]
        ordered = [
            sides[side][part * inner : (part + 1) * inner]
            for part in range(2)
            for side in range(halves)
        ]
        spare = by_round.shape[1] - 2 * width
        if spare:
            ordered.append(jnp.zeros((spare, half_count), jnp.float32))
        by_round[pl.ds(index, half_count, stride=padded_rounds), :] = (
            jnp.concatenate(ordered, axis=0).T * weight
        )

    backward_out[...] = by_round[...].astype(jnp.bfloat16).reshape(backward_out.shape)
    send(backward_out, backward_in, backward_sems)
    wait(backward_in, backward_sems.at[1])

    for pair in range(pairs):
        first = pair * padded_rounds
        arrived = (
            backward_in[...]
            .astype(jnp.float32)[:, first : first + padded_rounds]
            .reshape(ranks * padded_rounds, by_round.shape[1])
            .T
        )
        result = jnp.zeros((width, columns), jnp.float32)
        for part in range(2):
            result = result + jnp.dot(
                arrived[part * width : (part + 1) * width].astype(jnp.bfloat16),
                table[pair, :, part * columns : (part + 1) * columns],
                preferred_element_type=jnp.float32,
            )
        grid_ref[pair * width : (pair + 1) * width, 0:columns] = result.astype(jnp.bfloat16)
        if columns < grid_ref.shape[1]:
            grid_ref[pair * width : (pair + 1) * width, columns:] = jnp.zeros(
                (width, grid_ref.shape[1] - columns), jnp.bfloat16
            )

    basis_copy.wait_send()
    wait(forward_out, forward_sems.at[0])
    wait(backward_out, backward_sems.at[0])


def per_device(ranks, halves, grid_fields, legendre_basis, owner_list, wave_speed):
    fields, modes, pairs, hemis, padded = grid_fields.shape
    slots, _, half_count, totals = legendre_basis.shape
    wave_count = owner_list.shape[0]
    longest = 20 + 4 * (half_count - 1)
    highest = min(wave_count - 1, (longest - 1) // 2)
    rounds = min(slots, highest // ranks + 1)
    padded_rounds = round_up(rounds, 8)
    columns = min(padded, round_up(longest, 128))
    lanes = round_up(2 * hemis * fields * modes, 128)
    block_rows = pairs * padded_rounds
    sizes = (ranks, halves, slots, rounds, padded_rounds, fields, modes, pairs, wave_count)
    grid_rows = jnp.transpose(grid_fields, (2, 3, 0, 1, 4)).reshape(-1, padded)
    block = pltpu.VMEM((ranks, block_rows, lanes), jnp.bfloat16)
    spectra, rows = pl.pallas_call(
        functools.partial(kernel, sizes),
        out_shape=(
            pltpu.VMEM((rounds, 2 * fields * modes, totals), jnp.bfloat16),
            pltpu.VMEM(grid_rows.shape, jnp.bfloat16),
        ),
        in_specs=[pl.BlockSpec(memory_space=pltpu.VMEM)]
        + [pl.BlockSpec(memory_space=pltpu.HBM)] * 3,
        out_specs=[pl.BlockSpec(memory_space=pltpu.VMEM)] * 2,
        scratch_shapes=[
            pltpu.VMEM((pairs, ranks * padded_rounds, 2 * columns), jnp.bfloat16),
            pltpu.VMEM((hemis, rounds, half_count, totals), jnp.bfloat16),
            block,
            block,
            block,
            block,
            pltpu.VMEM((ranks * block_rows, lanes), jnp.float32),
            pltpu.SMEM(owner_list.shape, jnp.int32),
            pltpu.SMEM(wave_speed.shape, jnp.float32),
            pltpu.SemaphoreType.DMA,
            pltpu.SemaphoreType.DMA((2,)),
            pltpu.SemaphoreType.DMA((2,)),
            pltpu.SemaphoreType.DMA((2,)),
            pltpu.SemaphoreType.DMA((2,)),
        ],
        compiler_params=pltpu.CompilerParams(
            collective_id=0, has_side_effects=True, vmem_limit_bytes=48 * 2**20
        ),
    )(
        pltpu.with_memory_space_constraint(grid_rows, pltpu.VMEM),
        *(
            pltpu.with_memory_space_constraint(operand, pltpu.HBM)
            for operand in (legendre_basis, owner_list, wave_speed)
        ),
    )
    balanced = spectra.reshape(rounds, 2, fields, modes, totals)
    if rounds < slots:
        balanced = jnp.pad(balanced, ((0, slots - rounds),) + ((0, 0),) * 4)
    balanced_grid = jnp.transpose(
        rows.reshape(pairs, hemis, fields, modes, padded), (2, 3, 0, 1, 4)
    )
    return (balanced, balanced_grid)


def solution(mesh):
    placed = (P(None, "fld", "lat", None, None), P("lat", "fld", None, None), P(), P("fld"))
    return jax.shard_map(
        functools.partial(per_device, mesh.shape["lat"], mesh.shape["fld"]),
        mesh=mesh,
        in_specs=placed,
        out_specs=(P("lat", None, None, "fld", None), P(None, "fld", "lat", None, None)),
        check_vma=False,
    )
```

```python
import functools

import jax
import jax.numpy as jnp
from jax import lax
from jax.experimental import pallas as pl
from jax.experimental.pallas import tpu as pltpu
from jax.sharding import PartitionSpec as P

MESH = pl.DeviceIdType.MESH

COS_SERIES = (
    0.9999992251396179,
    -19.738981246948242,
    64.92865753173828,
    -85.27162170410156,
    58.79049301147461,
    -21.07110595703125,
)
SIN_SERIES = (
    6.283185005187988,
    -41.341590881347656,
    81.59994506835938,
    -76.61447143554688,
    41.3428840637207,
    -12.471243858337402,
)


def polynomial(series, argument):
    total = jnp.full_like(argument, series[-1])
    for coefficient in series[-2::-1]:
        total = total * argument + coefficient
    return total


def round_up(value, multiple):
    return -(-value // multiple) * multiple


def kernel(
    sizes,
    rows_ref,
    basis_ref,
    owner_hbm,
    speed_hbm,
    spectra_ref,
    grid_ref,
    table,
    placing,
    basis,
    forward_out,
    forward_in,
    backward_out,
    backward_in,
    by_round,
    owner_ref,
    speed_ref,
    own_sem,
    local_sems,
    basis_sems,
    all_sems,
    few_sems,
):
    (ranks, halves, slots, rounds, fields, modes, pairs, wave_count) = sizes
    inner = fields * modes
    width = halves * inner
    half_count = ranks * pairs
    waves, columns = table.shape[1], table.shape[2] // 2
    lanes = by_round.shape[1]
    pieces = forward_out.shape[0]
    per_piece = 8 // pairs
    totals = basis.shape[3]
    me = lax.axis_index("lat")
    hemisphere = lax.axis_index("fld")
    other = halves - 1 - hemisphere
    reach = [
        min(d for d in range(ranks) if largest(d * pairs + pairs - 1) >= g * per_piece * ranks)
        for g in range(pieces)
    ]

    own_copy = pltpu.make_async_copy(
        basis_ref.at[pl.ds(0, rounds), 0], basis.at[hemisphere], own_sem
    )
    owner_copy = pltpu.make_async_copy(owner_hbm, owner_ref, local_sems.at[0])
    speed_copy = pltpu.make_async_copy(speed_hbm, speed_ref, local_sems.at[1])
    owner_copy.start()
    speed_copy.start()
    own_copy.start()

    for g in range(1, pieces):
        forward_in[g] = jnp.zeros(forward_in.shape[1:], jnp.bfloat16)
        backward_in[g] = jnp.zeros(backward_in.shape[1:], jnp.bfloat16)

    barrier = pltpu.get_barrier_semaphore()

    def greet(step, carry):
        peer = lax.rem(me + step, ranks)
        pl.semaphore_signal(
            barrier, inc=1, device_id=(peer, hemisphere), device_id_type=MESH
        )
        return carry

    lax.fori_loop(1, ranks, greet, 0)
    pl.semaphore_signal(barrier, inc=1, device_id=(me, other), device_id_type=MESH)

    chunk = 16
    row_index = lax.broadcasted_iota(jnp.int32, (chunk, columns), 0)
    column = lax.broadcasted_iota(jnp.int32, (chunk, columns), 1)
    column_f = column.astype(jnp.float32)

    def fill(step, carry):
        wave = row_index + step * chunk
        product = wave.astype(jnp.float32) * column_f
        for pair in range(pairs):
            points = 20 + 4 * (me * pairs + pair)
            highest = jnp.minimum(wave_count - 1, (points - 1) // 2)
            points_f = jnp.full((1, columns), points, jnp.int32).astype(jnp.float32)
            inverse = 1.0 / points_f
            scaling = lax.rsqrt(points_f)
            turns = jnp.floor(product * inverse + 0.5)
            angle = (product - turns * points_f) * inverse
            square = angle * angle
            scale = jnp.where((column < points) & (wave <= highest), scaling, 0.0)
            cosine = polynomial(COS_SERIES, square) * scale
            sine = polynomial(SIN_SERIES, square) * (angle * scale)
            where = pl.ds(pl.multiple_of(step * chunk, chunk), chunk)
            table[pair, where, 0:columns] = cosine.astype(jnp.bfloat16)
            table[pair, where, columns : 2 * columns] = (-sine).astype(jnp.bfloat16)
        return carry

    lax.fori_loop(0, waves // chunk, fill, 0, unroll=waves // chunk <= 8)

    found = []
    for pair in range(pairs):
        values = rows_ref[pair * width : (pair + 1) * width, 0:columns]
        empty = jnp.zeros_like(values)
        both = [
            jnp.concatenate([values, empty], axis=1),
            jnp.concatenate([empty, values], axis=1),
        ]
        if lanes > 2 * width:
            both.append(jnp.zeros((lanes - 2 * width, 2 * columns), jnp.bfloat16))
        found.append(
            lax.dot_general(
                table[pair],
                jnp.concatenate(both, axis=0),
                (((1,), (1,)), ((), ())),
                preferred_element_type=jnp.float32,
            ).astype(jnp.bfloat16)
        )

    owner_copy.wait()
    place = lax.broadcasted_iota(jnp.int32, (8, waves), 0) % per_piece
    natural = lax.broadcasted_iota(jnp.int32, (8, waves), 1)
    for g in range(pieces):

        def choose(device, carry, g=g):
            wave = jnp.full((8, waves), -1, jnp.int32)
            for index in range(min(per_piece, rounds - g * per_piece)):
                number = owner_ref[device * slots + g * per_piece + index]
                wave = jnp.where(place == index, number, wave)
            where = pl.ds(pl.multiple_of((g * ranks + device) * 8, 8), 8)
            placing[where, :] = jnp.where(wave == natural, 1.0, 0.0)
            return carry

        lax.fori_loop(0, ranks, choose, 0, unroll=ranks <= 16)
    chosen = placing[...].astype(jnp.bfloat16)
    placed = jnp.dot(
        chosen, jnp.concatenate(found, axis=1), preferred_element_type=jnp.float32
    )
    block_rows = lax.broadcasted_iota(jnp.int32, (placed.shape[0], lanes), 0) % 8
    outgoing = placed[:, 0:lanes]
    for pair in range(1, pairs):
        outgoing = jnp.where(
            block_rows >= pair * per_piece,
            placed[:, pair * lanes : (pair + 1) * lanes],
            outgoing,
        )
    forward_out[...] = outgoing.reshape(forward_out.shape).astype(jnp.bfloat16)

    pl.semaphore_wait(barrier, ranks)

    def copy(out, into, g, peer, send_sem, recv_sem):
        return pltpu.make_async_remote_copy(
            src_ref=out.at[g, peer],
            dst_ref=into.at[g, me],
            send_sem=send_sem,
            recv_sem=recv_sem,
            device_id=(peer, hemisphere),
            device_id_type=MESH,
        )

    def send_all(out, into, g, send_sem, recv_sem_of):
        def one(step, carry):
            peer = lax.rem(me + step, ranks)
            copy(out, into, g, peer, send_sem, recv_sem_of).start()
            return carry

        lax.fori_loop(1, ranks, one, 0)

    def wait_all(ref, g, sem):
        part = ref.at[g, pl.ds(0, ranks - 1)]
        pltpu.make_async_copy(part, part, sem).wait()

    def each_far(g, act):
        def one(device, carry):
            @pl.when(device != me)
            def _():
                act(device)

            return carry

        lax.fori_loop(reach[g], ranks, one, 0)

    send_all(forward_out, forward_in, 0, all_sems.at[0, 0, 0], all_sems.at[0, 0, 1])
    for g in range(1, pieces):

        @pl.when(me >= reach[g])
        def _(g=g):
            send_all(forward_out, forward_in, g, all_sems.at[0, g, 0], few_sems.at[0, g, me])

    basis_copy = pltpu.make_async_remote_copy(
        src_ref=basis_ref.at[pl.ds(0, rounds), 0],
        dst_ref=basis.at[hemisphere],
        send_sem=basis_sems.at[0],
        recv_sem=basis_sems.at[1],
        device_id=(me, other),
        device_id_type=MESH,
    )
    basis_copy.start()
    for g in range(pieces):
        forward_in[g, me] = forward_out[g, me]

    speed_copy.wait()
    mode_index = lax.broadcasted_iota(jnp.int32, (modes, totals), 0)
    degree_i = lax.broadcasted_iota(jnp.int32, (modes, totals), 1)
    degree = degree_i.astype(jnp.float32)
    speeds = jnp.zeros((modes, totals), jnp.float32)
    for mode in range(modes):
        speeds = jnp.where(mode_index == mode, speed_ref[mode], speeds)
    stiffness = degree * (degree + 1.0) * speeds
    retained = 1.0 / (1.0 + stiffness)
    root_term = jnp.sqrt(stiffness)
    removed = stiffness * retained

    own_copy.wait()
    basis_copy.wait_recv()
    wait_all(forward_in, 0, all_sems.at[0, 0, 1])
    for g in range(1, pieces):
        each_far(
            g,
            lambda device, g=g: pltpu.make_async_copy(
                forward_in.at[g, device], forward_in.at[g, device], few_sems.at[0, g, device]
            ).wait(),
        )
    by_round[...] = forward_in[...].astype(jnp.float32).reshape(by_round.shape)

    def rows_of(index):
        first = (index // per_piece) * ranks * 8 + index % per_piece
        return pl.ds(first, half_count, stride=per_piece)

    incoming = [by_round[rows_of(index), :] for index in range(rounds)]
    by_round[...] = jnp.zeros_like(by_round)

    for index in range(rounds):
        number = owner_ref[me * slots + index]
        turned = incoming[index].T
        spectra = jnp.zeros((2 * inner, totals), jnp.float32)
        for side in range(halves):
            coefficients = jnp.concatenate(
                [
                    turned[part * width + side * inner : part * width + (side + 1) * inner]
                    for part in range(2)
                ],
                axis=0,
            ).astype(jnp.bfloat16)
            spectra = spectra + jnp.dot(
                coefficients, basis[side, index], preferred_element_type=jnp.float32
            )
        kept = degree_i >= number
        values = []
        for part in range(2):
            first = part * inner
            vorticity = spectra[first : first + modes]
            divergence = spectra[first + modes : first + 2 * modes]
            geopotential = spectra[first + 2 * modes : first + 3 * modes]
            rossby_part = (root_term * vorticity - geopotential) * retained
            for value in (
                retained * vorticity + removed * root_term * rossby_part,
                retained * divergence,
                retained * geopotential - removed * rossby_part,
            ):
                values.append(jnp.where(kept, value, 0.0))
        balanced = jnp.concatenate(values, axis=0).astype(jnp.bfloat16)
        spectra_ref[index] = balanced
        weight = jnp.where(number == 0, 1.0, 2.0)
        sides = [
            lax.dot_general(
                balanced,
                basis[side, index],
                (((1,), (1,)), ((), ())),
                preferred_element_type=jnp.float32,
            )
            for side in range(halves)
        ]
        ordered = [
            sides[side][part * inner : (part + 1) * inner]
            for part in range(2)
            for side in range(halves)
        ]
        if lanes > 2 * width:
            ordered.append(jnp.zeros((lanes - 2 * width, half_count), jnp.float32))
        by_round[rows_of(index), :] = jnp.concatenate(ordered, axis=0).T * weight

    backward_out[...] = by_round[...].reshape(backward_out.shape).astype(jnp.bfloat16)
    send_all(backward_out, backward_in, 0, all_sems.at[1, 0, 0], all_sems.at[1, 0, 1])
    for g in range(1, pieces):
        each_far(
            g,
            lambda device, g=g: copy(
                backward_out, backward_in, g, device, few_sems.at[1, g, device], all_sems.at[1, g, 1]
            ).start(),
        )
    for g in range(pieces):
        backward_in[g, me] = backward_out[g, me]
    wait_all(backward_in, 0, all_sems.at[1, 0, 1])
    for g in range(1, pieces):

        @pl.when(me >= reach[g])
        def _(g=g):
            wait_all(backward_in, g, all_sems.at[1, g, 1])

    arrived = backward_in[...].astype(jnp.float32).reshape(by_round.shape).T
    block_columns = lax.broadcasted_iota(jnp.int32, arrived.shape, 1) % 8
    by_pair = [
        jnp.where(block_columns // per_piece == pair, arrived, 0.0) for pair in range(pairs)
    ]
    ordered = jnp.dot(
        jnp.concatenate(by_pair, axis=0).astype(jnp.bfloat16),
        placing[...].astype(jnp.bfloat16),
        preferred_element_type=jnp.float32,
    )
    for pair in range(pairs):
        result = jnp.zeros((width, columns), jnp.float32)
        for part in range(2):
            first = pair * lanes + part * width
            result = result + jnp.dot(
                ordered[first : first + width].astype(jnp.bfloat16),
                table[pair, :, part * columns : (part + 1) * columns],
                preferred_element_type=jnp.float32,
            )
        grid_ref[pair * width : (pair + 1) * width, 0:columns] = result.astype(jnp.bfloat16)
        if columns < grid_ref.shape[1]:
            grid_ref[pair * width : (pair + 1) * width, columns:] = jnp.zeros(
                (width, grid_ref.shape[1] - columns), jnp.bfloat16
            )

    basis_copy.wait_send()
    for way, out in ((0, forward_out), (1, backward_out)):
        wait_all(out, 0, all_sems.at[way, 0, 0])
    for g in range(1, pieces):

        @pl.when(me >= reach[g])
        def _(g=g):
            wait_all(forward_out, g, all_sems.at[0, g, 0])

        each_far(
            g,
            lambda device, g=g: pltpu.make_async_copy(
                backward_out.at[g, device], backward_out.at[g, device], few_sems.at[1, g, device]
            ).wait(),
        )


def largest(pair_index):
    return (20 + 4 * pair_index - 1) // 2


def per_device(ranks, halves, grid_fields, legendre_basis, owner_list, wave_speed):
    fields, modes, pairs, hemis, padded = grid_fields.shape
    slots, _, half_count, totals = legendre_basis.shape
    wave_count = owner_list.shape[0]
    longest = 20 + 4 * (half_count - 1)
    highest = min(wave_count - 1, largest(half_count - 1))
    rounds = min(slots, highest // ranks + 1)
    pieces = round_up(rounds * pairs, 8) // 8
    waves = rounds * ranks
    columns = min(padded, round_up(longest, 128))
    lanes = round_up(2 * hemis * fields * modes, 128)
    sizes = (ranks, halves, slots, rounds, fields, modes, pairs, wave_count)
    grid_rows = jnp.transpose(grid_fields, (2, 3, 0, 1, 4)).reshape(-1, padded)
    block = pltpu.VMEM((pieces, ranks, 8, lanes), jnp.bfloat16)
    spectra, rows = pl.pallas_call(
        functools.partial(kernel, sizes),
        out_shape=(
            pltpu.VMEM((rounds, 2 * fields * modes, totals), jnp.bfloat16),
            pltpu.VMEM(grid_rows.shape, jnp.bfloat16),
        ),
        in_specs=[pl.BlockSpec(memory_space=pltpu.VMEM)]
        + [pl.BlockSpec(memory_space=pltpu.HBM)] * 3,
        out_specs=[pl.BlockSpec(memory_space=pltpu.VMEM)] * 2,
        scratch_shapes=[
            pltpu.VMEM((pairs, waves, 2 * columns), jnp.bfloat16),
            pltpu.VMEM((pieces * ranks * 8, waves), jnp.float32),
            pltpu.VMEM((hemis, rounds, half_count, totals), jnp.bfloat16),
            block,
            block,
            block,
            block,
            pltpu.VMEM((pieces * ranks * 8, lanes), jnp.float32),
            pltpu.SMEM(owner_list.shape, jnp.int32),
            pltpu.SMEM(wave_speed.shape, jnp.float32),
            pltpu.SemaphoreType.DMA,
            pltpu.SemaphoreType.DMA((2,)),
            pltpu.SemaphoreType.DMA((2,)),
            pltpu.SemaphoreType.DMA((2, pieces, 2)),
            pltpu.SemaphoreType.DMA((2, pieces, ranks)),
        ],
        compiler_params=pltpu.CompilerParams(
            collective_id=0, has_side_effects=True, vmem_limit_bytes=48 * 2**20
        ),
    )(
        pltpu.with_memory_space_constraint(grid_rows, pltpu.VMEM),
        *(
            pltpu.with_memory_space_constraint(operand, pltpu.HBM)
            for operand in (legendre_basis, owner_list, wave_speed)
        ),
    )
    balanced = spectra.reshape(rounds, 2, fields, modes, totals)
    if rounds < slots:
        balanced = jnp.pad(balanced, ((0, slots - rounds),) + ((0, 0),) * 4)
    balanced_grid = jnp.transpose(
        rows.reshape(pairs, hemis, fields, modes, padded), (2, 3, 0, 1, 4)
    )
    return (balanced, balanced_grid)


def solution(mesh):
    placed = (P(None, "fld", "lat", None, None), P("lat", "fld", None, None), P(), P("fld"))
    return jax.shard_map(
        functools.partial(per_device, mesh.shape["lat"], mesh.shape["fld"]),
        mesh=mesh,
        in_specs=placed,
        out_specs=(P("lat", None, None, "fld", None), P(None, "fld", "lat", None, None)),
        check_vma=False,
    )
```

```python
import functools

import jax
import jax.numpy as jnp
from jax import lax
from jax.experimental import pallas as pl
from jax.experimental.pallas import tpu as pltpu
from jax.sharding import PartitionSpec as P

MESH = pl.DeviceIdType.MESH

COS_SERIES = (
    0.9999992251396179,
    -19.738981246948242,
    64.92865753173828,
    -85.27162170410156,
    58.79049301147461,
    -21.07110595703125,
)
SIN_SERIES = (
    6.283185005187988,
    -41.341590881347656,
    81.59994506835938,
    -76.61447143554688,
    41.3428840637207,
    -12.471243858337402,
)


def polynomial(series, argument):
    total = jnp.full_like(argument, series[-1])
    for coefficient in series[-2::-1]:
        total = total * argument + coefficient
    return total


def round_up(value, multiple):
    return -(-value // multiple) * multiple


def kernel(
    sizes,
    grid_hbm,
    basis_ref,
    owner_hbm,
    speed_hbm,
    spectra_ref,
    arrived_ref,
    table,
    grid_ref,
    lines,
    basis,
    forward_out,
    forward_in,
    backward_out,
    backward_in,
    by_round,
    owner_ref,
    speed_ref,
    own_sem,
    local_sems,
    basis_sems,
    forward_sems,
    backward_sems,
):
    (ranks, halves, slots, rounds, padded_rounds, fields, modes, pairs, wave_count) = sizes
    inner = fields * modes
    half_count = ranks * pairs
    columns = table.shape[2] // 2
    totals = basis.shape[3]
    me = lax.axis_index("lat")
    hemisphere = lax.axis_index("fld")
    other = halves - 1 - hemisphere

    barrier = pltpu.get_barrier_semaphore()

    def greet(step, carry):
        peer = lax.rem(me + step, ranks)
        pl.semaphore_signal(
            barrier, inc=1, device_id=(peer, hemisphere), device_id_type=MESH
        )
        return carry

    lax.fori_loop(1, ranks, greet, 0)
    pl.semaphore_signal(barrier, inc=1, device_id=(me, other), device_id_type=MESH)

    own_copy = pltpu.make_async_copy(
        basis_ref.at[pl.ds(0, rounds), 0], basis.at[hemisphere], own_sem
    )
    owner_copy = pltpu.make_async_copy(owner_hbm, owner_ref, local_sems.at[0])
    speed_copy = pltpu.make_async_copy(speed_hbm, speed_ref, local_sems.at[1])
    grid_copy = pltpu.make_async_copy(grid_hbm, grid_ref, local_sems.at[2])
    owner_copy.start()
    grid_copy.start()
    speed_copy.start()
    own_copy.start()

    together = max(1, 16 // padded_rounds)
    chunk = together * padded_rounds
    row_index = lax.broadcasted_iota(jnp.int32, (chunk, columns), 0)
    column = lax.broadcasted_iota(jnp.int32, (chunk, columns), 1)
    column_f = column.astype(jnp.float32)

    def fill(step, carry):
        wave = jnp.full((chunk, columns), -1, jnp.int32)
        for part in range(together):
            for index in range(rounds):
                number = owner_ref[(step * together + part) * slots + index]
                wave = jnp.where(row_index == part * padded_rounds + index, number, wave)
        product = wave.astype(jnp.float32) * column_f
        for pair in range(pairs):
            points = 20 + 4 * (me * pairs + pair)
            highest = jnp.minimum(wave_count - 1, (points - 1) // 2)
            points_f = jnp.full((1, columns), points, jnp.int32).astype(jnp.float32)
            inverse = 1.0 / points_f
            scaling = lax.rsqrt(points_f)
            turns = jnp.floor(product * inverse + 0.5)
            angle = (product - turns * points_f) * inverse
            square = angle * angle
            inside = (column < points) & (wave <= highest) & (wave >= 0)
            scale = jnp.where(inside, scaling, 0.0)
            cosine = polynomial(COS_SERIES, square) * scale
            sine = polynomial(SIN_SERIES, square) * (angle * scale)
            where = pl.ds(pl.multiple_of(step * chunk, chunk), chunk)
            table[pair, where, 0:columns] = cosine.astype(jnp.bfloat16)
            table[pair, where, columns : 2 * columns] = (-sine).astype(jnp.bfloat16)
        return carry

    owner_copy.wait()
    lax.fori_loop(0, ranks // together, fill, 0, unroll=2)

    grid_copy.wait()
    loaded = grid_ref[...].astype(jnp.float32).reshape(lines.shape[1], -1)
    for tile in range(columns // 128):
        lines[tile] = loaded[:, tile * 128 : (tile + 1) * 128]
    blocks = []
    width = halves * inner
    for pair in range(pairs):
        values = jnp.concatenate(
            [
                jnp.concatenate(
                    [
                        lines[tile, pl.ds(pair * halves + side, inner, stride=pairs * halves), :]
                        for tile in range(columns // 128)
                    ],
                    axis=1,
                )
                for side in range(halves)
            ],
            axis=0,
        ).astype(jnp.bfloat16)
        empty = jnp.zeros_like(values)
        both = jnp.concatenate(
            [
                jnp.concatenate([values, empty], axis=1),
                jnp.concatenate([empty, values], axis=1),
            ],
            axis=0,
        )
        found = lax.dot_general(
            table[pair], both, (((1,), (1,)), ((), ())), preferred_element_type=jnp.float32
        )
        blocks.append(found.reshape(ranks, padded_rounds, 2 * width))
    forward_out[:, :, 0 : 2 * width] = jnp.concatenate(blocks, axis=1).astype(jnp.bfloat16)

    pl.semaphore_wait(barrier, ranks)

    def send(out, into, sems):
        def one(step, carry):
            peer = lax.rem(me + step, ranks)
            pltpu.make_async_remote_copy(
                src_ref=out.at[peer],
                dst_ref=into.at[me],
                send_sem=sems.at[0],
                recv_sem=sems.at[1],
                device_id=(peer, hemisphere),
                device_id_type=MESH,
            ).start()
            return carry

        lax.fori_loop(1, ranks, one, 0)
        into[me] = out[me]

    def wait(ref, sem):
        part = ref.at[pl.ds(0, ranks - 1)]
        pltpu.make_async_copy(part, part, sem).wait()

    send(forward_out, forward_in, forward_sems)
    basis_copy = pltpu.make_async_remote_copy(
        src_ref=basis_ref.at[pl.ds(0, rounds), 0],
        dst_ref=basis.at[hemisphere],
        send_sem=basis_sems.at[0],
        recv_sem=basis_sems.at[1],
        device_id=(me, other),
        device_id_type=MESH,
    )
    basis_copy.start()

    speed_copy.wait()
    mode_index = lax.broadcasted_iota(jnp.int32, (modes, totals), 0)
    degree_i = lax.broadcasted_iota(jnp.int32, (modes, totals), 1)
    degree = degree_i.astype(jnp.float32)
    speeds = jnp.zeros((modes, totals), jnp.float32)
    for mode in range(modes):
        speeds = jnp.where(mode_index == mode, speed_ref[mode], speeds)
    stiffness = degree * (degree + 1.0) * speeds
    retained = 1.0 / (1.0 + stiffness)
    root_term = jnp.sqrt(stiffness)
    removed = stiffness * retained

    wait(forward_in, forward_sems.at[1])
    by_round[...] = forward_in[...].astype(jnp.float32).reshape(by_round.shape)
    own_copy.wait()
    basis_copy.wait_recv()

    incoming = [
        by_round[pl.ds(index, half_count, stride=padded_rounds), :] for index in range(rounds)
    ]
    by_round[...] = jnp.zeros_like(by_round)

    for index in range(rounds):
        number = owner_ref[me * slots + index]
        turned = incoming[index].T
        spectra = jnp.zeros((2 * inner, totals), jnp.float32)
        for side in range(halves):
            coefficients = jnp.concatenate(
                [
                    turned[part * width + side * inner : part * width + (side + 1) * inner]
                    for part in range(2)
                ],
                axis=0,
            ).astype(jnp.bfloat16)
            spectra = spectra + jnp.dot(
                coefficients, basis[side, index], preferred_element_type=jnp.float32
            )
        kept = degree_i >= number
        pieces = []
        for part in range(2):
            first = part * inner
            vorticity = spectra[first : first + modes]
            divergence = spectra[first + modes : first + 2 * modes]
            geopotential = spectra[first + 2 * modes : first + 3 * modes]
            rossby_part = (root_term * vorticity - geopotential) * retained
            for value in (
                retained * vorticity + removed * root_term * rossby_part,
                retained * divergence,
                retained * geopotential - removed * rossby_part,
            ):
                pieces.append(jnp.where(kept, value, 0.0))
        balanced = jnp.concatenate(pieces, axis=0).astype(jnp.bfloat16)
        spectra_ref[index] = balanced
        weight = jnp.where(number == 0, 1.0, 2.0)
        sides = [
            lax.dot_general(
                balanced,
                basis[side, index],
                (((1,), (1,)), ((), ())),
                preferred_element_type=jnp.float32,
            )
            for side in range(halves)
        ]
        ordered = [
            sides[side][part * inner : (part + 1) * inner]
            for part in range(2)
            for side in range(halves)
        ]
        spare = by_round.shape[1] - 2 * width
        if spare:
            ordered.append(jnp.zeros((spare, half_count), jnp.float32))
        by_round[pl.ds(index, half_count, stride=padded_rounds), :] = (
            jnp.concatenate(ordered, axis=0).T * weight
        )

    backward_out[...] = by_round[...].astype(jnp.bfloat16).reshape(backward_out.shape)
    send(backward_out, backward_in, backward_sems)
    wait(backward_in, backward_sems.at[1])

    arrived_ref[...] = backward_in[...]

    basis_copy.wait_send()
    wait(forward_out, forward_sems.at[0])
    wait(backward_out, backward_sems.at[0])


def finish(
    sizes,
    arrived_ref,
    table,
    spectra_ref,
    balanced_hbm,
    grid_hbm,
    zeros,
    lines,
    grid_ref,
    copy_sems,
):
    ranks, halves, slots, rounds, padded_rounds, inner, pairs = sizes
    columns = table.shape[2] // 2
    width = halves * inner
    copies = [
        pltpu.make_async_copy(
            spectra_ref, balanced_hbm.at[pl.ds(0, rounds)], copy_sems.at[0]
        )
    ]
    copies[0].start()
    if rounds < slots:
        zeros[...] = jnp.zeros_like(zeros)
    for start in range(rounds, slots, rounds):
        count = min(rounds, slots - start)
        copies.append(
            pltpu.make_async_copy(
                zeros.at[pl.ds(0, count)],
                balanced_hbm.at[pl.ds(start, count)],
                copy_sems.at[len(copies)],
            )
        )
        copies[-1].start()

    for tile in range(columns // 128, lines.shape[0]):
        lines[tile] = jnp.zeros(lines.shape[1:], jnp.float32)
    for pair in range(pairs):
        first = pair * padded_rounds
        arrived = (
            arrived_ref[...]
            .astype(jnp.float32)[:, first : first + padded_rounds]
            .reshape(ranks * padded_rounds, arrived_ref.shape[2])
            .T
        )
        result = jnp.zeros((width, columns), jnp.float32)
        for part in range(2):
            result = result + jnp.dot(
                arrived[part * width : (part + 1) * width].astype(jnp.bfloat16),
                table[pair, :, part * columns : (part + 1) * columns],
                preferred_element_type=jnp.float32,
            )
        for side in range(halves):
            where = pl.ds(pair * halves + side, inner, stride=pairs * halves)
            for tile in range(columns // 128):
                lines[tile, where, :] = result[
                    side * inner : (side + 1) * inner, tile * 128 : (tile + 1) * 128
                ]
    joined = jnp.concatenate([lines[tile] for tile in range(lines.shape[0])], axis=1)
    grid_ref[...] = joined.reshape(grid_ref.shape).astype(jnp.bfloat16)
    copies.append(pltpu.make_async_copy(grid_ref, grid_hbm, copy_sems.at[len(copies)]))
    copies[-1].start()
    for one in copies:
        one.wait()


def per_device(ranks, halves, grid_fields, legendre_basis, owner_list, wave_speed):
    fields, modes, pairs, hemis, padded = grid_fields.shape
    slots, _, half_count, totals = legendre_basis.shape
    wave_count = owner_list.shape[0]
    longest = 20 + 4 * (half_count - 1)
    highest = min(wave_count - 1, (longest - 1) // 2)
    rounds = min(slots, highest // ranks + 1)
    padded_rounds = round_up(rounds, 8)
    columns = min(padded, round_up(longest, 128))
    lanes = round_up(2 * hemis * fields * modes, 128)
    block_rows = pairs * padded_rounds
    sizes = (ranks, halves, slots, rounds, padded_rounds, fields, modes, pairs, wave_count)
    table_shape = (pairs, ranks * padded_rounds, 2 * columns)
    block = pltpu.VMEM((ranks, block_rows, lanes), jnp.bfloat16)
    line_scratch = [
        pltpu.VMEM(grid_fields.shape, jnp.bfloat16),
        pltpu.VMEM((padded // 128, fields * modes * pairs * hemis, 128), jnp.float32),
    ]
    spectra_shape = (rounds, 2 * fields * modes, totals)
    spectra, arrived, table = pl.pallas_call(
        functools.partial(kernel, sizes),
        out_shape=(
            pltpu.VMEM(spectra_shape, jnp.bfloat16),
            block,
            pltpu.VMEM(table_shape, jnp.bfloat16),
        ),
        in_specs=[pl.BlockSpec(memory_space=pltpu.HBM)] * 4,
        out_specs=[pl.BlockSpec(memory_space=pltpu.VMEM)] * 3,
        scratch_shapes=line_scratch
        + [
            pltpu.VMEM((hemis, rounds, half_count, totals), jnp.bfloat16),
            block,
            block,
            block,
            block,
            pltpu.VMEM((ranks * block_rows, lanes), jnp.float32),
            pltpu.SMEM(owner_list.shape, jnp.int32),
            pltpu.SMEM(wave_speed.shape, jnp.float32),
            pltpu.SemaphoreType.DMA,
            pltpu.SemaphoreType.DMA((3,)),
            pltpu.SemaphoreType.DMA((2,)),
            pltpu.SemaphoreType.DMA((2,)),
            pltpu.SemaphoreType.DMA((2,)),
        ],
        compiler_params=pltpu.CompilerParams(
            collective_id=0, has_side_effects=True, vmem_limit_bytes=40 * 2**20
        ),
    )(
        *(
            pltpu.with_memory_space_constraint(operand, pltpu.HBM)
            for operand in (grid_fields, legendre_basis, owner_list, wave_speed)
        ),
    )
    copies = 2 + -(-(slots - rounds) // rounds)
    balanced, balanced_grid = pl.pallas_call(
        functools.partial(
            finish, (ranks, halves, slots, rounds, padded_rounds, fields * modes, pairs)
        ),
        out_shape=(
            pltpu.HBM((slots,) + spectra_shape[1:], jnp.bfloat16),
            pltpu.HBM(grid_fields.shape, jnp.bfloat16),
        ),
        in_specs=[pl.BlockSpec(memory_space=pltpu.VMEM)] * 3,
        out_specs=[pl.BlockSpec(memory_space=pltpu.HBM)] * 2,
        scratch_shapes=[pltpu.VMEM(spectra_shape, jnp.bfloat16)]
        + line_scratch[::-1]
        + [pltpu.SemaphoreType.DMA((copies,))],
        compiler_params=pltpu.CompilerParams(vmem_limit_bytes=40 * 2**20),
    )(
        *(
            pltpu.with_memory_space_constraint(operand, pltpu.VMEM)
            for operand in (arrived, table, spectra)
        ),
    )
    return (balanced.reshape(slots, 2, fields, modes, totals), balanced_grid)


def solution(mesh):
    placed = (P(None, "fld", "lat", None, None), P("lat", "fld", None, None), P(), P("fld"))
    return jax.shard_map(
        functools.partial(per_device, mesh.shape["lat"], mesh.shape["fld"]),
        mesh=mesh,
        in_specs=placed,
        out_specs=(P("lat", None, None, "fld", None), P(None, "fld", "lat", None, None)),
        check_vma=False,
    )
```

```python
import functools

import jax
import jax.numpy as jnp
from jax import lax
from jax.experimental import pallas as pl
from jax.experimental.pallas import tpu as pltpu
from jax.sharding import PartitionSpec as P

MESH = pl.DeviceIdType.MESH

COS_SERIES = (
    0.9999992251396179,
    -19.738981246948242,
    64.92865753173828,
    -85.27162170410156,
    58.79049301147461,
    -21.07110595703125,
)
SIN_SERIES = (
    6.283185005187988,
    -41.341590881347656,
    81.59994506835938,
    -76.61447143554688,
    41.3428840637207,
    -12.471243858337402,
)


def polynomial(series, argument):
    total = jnp.full_like(argument, series[-1])
    for coefficient in series[-2::-1]:
        total = total * argument + coefficient
    return total


def round_up(value, multiple):
    return -(-value // multiple) * multiple


def for_partners(me, ranks, act):
    bits = ranks.bit_length() - 1
    if ranks != 1 << bits:

        def around(step, carry):
            act(lax.rem(me + step, ranks))
            return carry

        lax.fori_loop(1, ranks, around, 0)
        return
    flips = [(1 - 2 * ((me // (1 << bit)) % 2)) * (1 << bit) for bit in range(bits)]
    if ranks <= 16:
        for step in range(ranks - 1, 0, -1):
            act(me + sum(flips[bit] for bit in range(bits) if step >> bit & 1))
        return

    def across(index, carry):
        step = ranks - 1 - index
        act(me + sum(flips[bit] * ((step // (1 << bit)) % 2) for bit in range(bits)))
        return carry

    lax.fori_loop(0, ranks - 1, across, 0)


def kernel(
    sizes,
    grid_hbm,
    basis_ref,
    owner_hbm,
    speed_hbm,
    spectra_ref,
    arrived_ref,
    table,
    grid_ref,
    lines,
    basis,
    forward_out,
    forward_in,
    backward_out,
    backward_in,
    by_round,
    owner_ref,
    speed_ref,
    own_sem,
    local_sems,
    basis_sems,
    forward_sems,
    backward_sems,
):
    (ranks, halves, slots, rounds, padded_rounds, fields, modes, pairs, wave_count) = sizes
    inner = fields * modes
    half_count = ranks * pairs
    columns = table.shape[2] // 2
    totals = basis.shape[2]
    me = lax.axis_index("lat")
    hemisphere = lax.axis_index("fld")
    other = halves - 1 - hemisphere

    barrier = pltpu.get_barrier_semaphore()

    for_partners(
        me,
        ranks,
        lambda peer: pl.semaphore_signal(
            barrier, inc=1, device_id=(peer, hemisphere), device_id_type=MESH
        ),
    )
    pl.semaphore_signal(barrier, inc=1, device_id=(me, other), device_id_type=MESH)

    own_side = basis.at[
        :, pl.ds(pl.multiple_of(hemisphere * half_count, half_count), half_count)
    ]
    own_copy = pltpu.make_async_copy(
        basis_ref.at[pl.ds(0, rounds), 0], own_side, own_sem
    )
    owner_copy = pltpu.make_async_copy(owner_hbm, owner_ref, local_sems.at[0])
    speed_copy = pltpu.make_async_copy(speed_hbm, speed_ref, local_sems.at[1])
    grid_copy = pltpu.make_async_copy(grid_hbm, grid_ref, local_sems.at[2])
    owner_copy.start()
    grid_copy.start()
    speed_copy.start()
    own_copy.start()

    together = max(1, 16 // padded_rounds)
    chunk = together * padded_rounds
    row_index = lax.broadcasted_iota(jnp.int32, (chunk, columns), 0)
    column = lax.broadcasted_iota(jnp.int32, (chunk, columns), 1)
    column_f = column.astype(jnp.float32)

    def fill(step, carry):
        wave = jnp.full((chunk, columns), -1, jnp.int32)
        for part in range(together):
            for index in range(rounds):
                number = owner_ref[(step * together + part) * slots + index]
                wave = jnp.where(row_index == part * padded_rounds + index, number, wave)
        product = wave.astype(jnp.float32) * column_f
        for pair in range(pairs):
            points = 20 + 4 * (me * pairs + pair)
            highest = jnp.minimum(wave_count - 1, (points - 1) // 2)
            points_f = jnp.full((1, columns), points, jnp.int32).astype(jnp.float32)
            inverse = 1.0 / points_f
            scaling = lax.rsqrt(points_f)
            turns = jnp.floor(product * inverse + 0.5)
            angle = (product - turns * points_f) * inverse
            square = angle * angle
            inside = (column < points) & (wave <= highest) & (wave >= 0)
            scale = jnp.where(inside, scaling, 0.0)
            cosine = polynomial(COS_SERIES, square) * scale
            sine = polynomial(SIN_SERIES, square) * (angle * scale)
            where = pl.ds(pl.multiple_of(step * chunk, chunk), chunk)
            table[pair, where, 0:columns] = cosine.astype(jnp.bfloat16)
            table[pair, where, columns : 2 * columns] = (-sine).astype(jnp.bfloat16)
        return carry

    owner_copy.wait()
    lax.fori_loop(0, ranks // together, fill, 0, unroll=2)

    grid_copy.wait()
    loaded = grid_ref[...].astype(jnp.float32).reshape(lines.shape[1], -1)
    for tile in range(columns // 128):
        lines[tile] = loaded[:, tile * 128 : (tile + 1) * 128]
    blocks = []
    width = halves * inner
    for pair in range(pairs):
        values = jnp.concatenate(
            [
                jnp.concatenate(
                    [
                        lines[tile, pl.ds(pair * halves + side, inner, stride=pairs * halves), :]
                        for tile in range(columns // 128)
                    ],
                    axis=1,
                )
                for side in range(halves)
            ],
            axis=0,
        ).astype(jnp.bfloat16)
        empty = jnp.zeros_like(values)
        both = jnp.concatenate(
            [
                jnp.concatenate([values, empty], axis=1),
                jnp.concatenate([empty, values], axis=1),
            ],
            axis=0,
        )
        found = lax.dot_general(
            table[pair], both, (((1,), (1,)), ((), ())), preferred_element_type=jnp.float32
        )
        blocks.append(found.reshape(ranks, padded_rounds, 2 * width))
    forward_out[:, :, 0 : 2 * width] = jnp.concatenate(blocks, axis=1).astype(jnp.bfloat16)

    pl.semaphore_wait(barrier, ranks)

    def send(out, into, sems):
        def one(peer):
            pltpu.make_async_remote_copy(
                src_ref=out.at[peer],
                dst_ref=into.at[me],
                send_sem=sems.at[0],
                recv_sem=sems.at[1],
                device_id=(peer, hemisphere),
                device_id_type=MESH,
            ).start()

        for_partners(me, ranks, one)
        into[me] = out[me]

    def wait(ref, sem):
        part = ref.at[pl.ds(0, ranks - 1)]
        pltpu.make_async_copy(part, part, sem).wait()

    send(forward_out, forward_in, forward_sems)
    basis_copy = pltpu.make_async_remote_copy(
        src_ref=basis_ref.at[pl.ds(0, rounds), 0],
        dst_ref=own_side,
        send_sem=basis_sems.at[0],
        recv_sem=basis_sems.at[1],
        device_id=(me, other),
        device_id_type=MESH,
    )
    basis_copy.start()

    speed_copy.wait()
    mode_index = lax.broadcasted_iota(jnp.int32, (modes, totals), 0)
    degree_i = lax.broadcasted_iota(jnp.int32, (modes, totals), 1)
    degree = degree_i.astype(jnp.float32)
    speeds = jnp.zeros((modes, totals), jnp.float32)
    for mode in range(modes):
        speeds = jnp.where(mode_index == mode, speed_ref[mode], speeds)
    stiffness = degree * (degree + 1.0) * speeds
    retained = 1.0 / (1.0 + stiffness)
    root_term = jnp.sqrt(stiffness)
    removed = stiffness * retained

    wait(forward_in, forward_sems.at[1])
    by_round[...] = forward_in[...].astype(jnp.float32).reshape(by_round.shape)
    own_copy.wait()
    basis_copy.wait_recv()

    incoming = [
        by_round[pl.ds(index, half_count, stride=padded_rounds), :] for index in range(rounds)
    ]
    by_round[...] = jnp.zeros_like(by_round)

    for index in range(rounds):
        number = owner_ref[me * slots + index]
        turned = incoming[index].T
        coefficients = jnp.concatenate(
            [
                jnp.concatenate(
                    [
                        turned[part * width + side * inner : part * width + (side + 1) * inner]
                        for part in range(2)
                    ],
                    axis=0,
                )
                for side in range(halves)
            ],
            axis=1,
        ).astype(jnp.bfloat16)
        spectra = jnp.dot(coefficients, basis[index], preferred_element_type=jnp.float32)
        kept = degree_i >= number
        pieces = []
        for part in range(2):
            first = part * inner
            vorticity = spectra[first : first + modes]
            divergence = spectra[first + modes : first + 2 * modes]
            geopotential = spectra[first + 2 * modes : first + 3 * modes]
            rossby_part = (root_term * vorticity - geopotential) * retained
            for value in (
                retained * vorticity + removed * root_term * rossby_part,
                retained * divergence,
                retained * geopotential - removed * rossby_part,
            ):
                pieces.append(jnp.where(kept, value, 0.0))
        balanced = jnp.concatenate(pieces, axis=0).astype(jnp.bfloat16)
        spectra_ref[index] = balanced
        weight = jnp.where(number == 0, 1.0, 2.0)
        returned = lax.dot_general(
            balanced, basis[index], (((1,), (1,)), ((), ())), preferred_element_type=jnp.float32
        )
        ordered = [
            returned[
                part * inner : (part + 1) * inner, side * half_count : (side + 1) * half_count
            ]
            for part in range(2)
            for side in range(halves)
        ]
        spare = by_round.shape[1] - 2 * width
        if spare:
            ordered.append(jnp.zeros((spare, half_count), jnp.float32))
        by_round[pl.ds(index, half_count, stride=padded_rounds), :] = (
            jnp.concatenate(ordered, axis=0).T * weight
        )

    backward_out[...] = by_round[...].astype(jnp.bfloat16).reshape(backward_out.shape)
    send(backward_out, backward_in, backward_sems)
    wait(backward_in, backward_sems.at[1])

    arrived_ref[...] = backward_in[...]

    basis_copy.wait_send()
    wait(forward_out, forward_sems.at[0])
    wait(backward_out, backward_sems.at[0])


def finish(
    sizes,
    arrived_ref,
    table,
    spectra_ref,
    balanced_hbm,
    grid_hbm,
    zeros,
    lines,
    grid_ref,
    copy_sems,
):
    ranks, halves, slots, rounds, padded_rounds, inner, pairs = sizes
    columns = table.shape[2] // 2
    width = halves * inner
    copies = [
        pltpu.make_async_copy(
            spectra_ref, balanced_hbm.at[pl.ds(0, rounds)], copy_sems.at[0]
        )
    ]
    copies[0].start()
    if rounds < slots:
        zeros[...] = jnp.zeros_like(zeros)
    for start in range(rounds, slots, rounds):
        count = min(rounds, slots - start)
        copies.append(
            pltpu.make_async_copy(
                zeros.at[pl.ds(0, count)],
                balanced_hbm.at[pl.ds(start, count)],
                copy_sems.at[len(copies)],
            )
        )
        copies[-1].start()

    for tile in range(columns // 128, lines.shape[0]):
        lines[tile] = jnp.zeros(lines.shape[1:], jnp.float32)
    for pair in range(pairs):
        first = pair * padded_rounds
        arrived = (
            arrived_ref[...]
            .astype(jnp.float32)[:, first : first + padded_rounds]
            .reshape(ranks * padded_rounds, arrived_ref.shape[2])
            .T
        )
        result = jnp.zeros((width, columns), jnp.float32)
        for part in range(2):
            result = result + jnp.dot(
                arrived[part * width : (part + 1) * width].astype(jnp.bfloat16),
                table[pair, :, part * columns : (part + 1) * columns],
                preferred_element_type=jnp.float32,
            )
        for side in range(halves):
            where = pl.ds(pair * halves + side, inner, stride=pairs * halves)
            for tile in range(columns // 128):
                lines[tile, where, :] = result[
                    side * inner : (side + 1) * inner, tile * 128 : (tile + 1) * 128
                ]
    joined = jnp.concatenate([lines[tile] for tile in range(lines.shape[0])], axis=1)
    grid_ref[...] = joined.reshape(grid_ref.shape).astype(jnp.bfloat16)
    copies.append(pltpu.make_async_copy(grid_ref, grid_hbm, copy_sems.at[len(copies)]))
    copies[-1].start()
    for one in copies:
        one.wait()


def per_device(ranks, halves, grid_fields, legendre_basis, owner_list, wave_speed):
    fields, modes, pairs, hemis, padded = grid_fields.shape
    slots, _, half_count, totals = legendre_basis.shape
    wave_count = owner_list.shape[0]
    longest = 20 + 4 * (half_count - 1)
    highest = min(wave_count - 1, (longest - 1) // 2)
    rounds = min(slots, highest // ranks + 1)
    padded_rounds = round_up(rounds, 8)
    columns = min(padded, round_up(longest, 128))
    lanes = round_up(2 * hemis * fields * modes, 128)
    block_rows = pairs * padded_rounds
    sizes = (ranks, halves, slots, rounds, padded_rounds, fields, modes, pairs, wave_count)
    table_shape = (pairs, ranks * padded_rounds, 2 * columns)
    block = pltpu.VMEM((ranks, block_rows, lanes), jnp.bfloat16)
    line_scratch = [
        pltpu.VMEM(grid_fields.shape, jnp.bfloat16),
        pltpu.VMEM((padded // 128, fields * modes * pairs * hemis, 128), jnp.float32),
    ]
    spectra_shape = (rounds, 2 * fields * modes, totals)
    spectra, arrived, table = pl.pallas_call(
        functools.partial(kernel, sizes),
        out_shape=(
            pltpu.VMEM(spectra_shape, jnp.bfloat16),
            block,
            pltpu.VMEM(table_shape, jnp.bfloat16),
        ),
        in_specs=[pl.BlockSpec(memory_space=pltpu.HBM)] * 4,
        out_specs=[pl.BlockSpec(memory_space=pltpu.VMEM)] * 3,
        scratch_shapes=line_scratch
        + [
            pltpu.VMEM((rounds, hemis * half_count, totals), jnp.bfloat16),
            block,
            block,
            block,
            block,
            pltpu.VMEM((ranks * block_rows, lanes), jnp.float32),
            pltpu.SMEM(owner_list.shape, jnp.int32),
            pltpu.SMEM(wave_speed.shape, jnp.float32),
            pltpu.SemaphoreType.DMA,
            pltpu.SemaphoreType.DMA((3,)),
            pltpu.SemaphoreType.DMA((2,)),
            pltpu.SemaphoreType.DMA((2,)),
            pltpu.SemaphoreType.DMA((2,)),
        ],
        compiler_params=pltpu.CompilerParams(
            collective_id=0, has_side_effects=True, vmem_limit_bytes=40 * 2**20
        ),
    )(
        *(
            pltpu.with_memory_space_constraint(operand, pltpu.HBM)
            for operand in (grid_fields, legendre_basis, owner_list, wave_speed)
        ),
    )
    copies = 2 + -(-(slots - rounds) // rounds)
    balanced, balanced_grid = pl.pallas_call(
        functools.partial(
            finish, (ranks, halves, slots, rounds, padded_rounds, fields * modes, pairs)
        ),
        out_shape=(
            pltpu.HBM((slots,) + spectra_shape[1:], jnp.bfloat16),
            pltpu.HBM(grid_fields.shape, jnp.bfloat16),
        ),
        in_specs=[pl.BlockSpec(memory_space=pltpu.VMEM)] * 3,
        out_specs=[pl.BlockSpec(memory_space=pltpu.HBM)] * 2,
        scratch_shapes=[pltpu.VMEM(spectra_shape, jnp.bfloat16)]
        + line_scratch[::-1]
        + [pltpu.SemaphoreType.DMA((copies,))],
        compiler_params=pltpu.CompilerParams(vmem_limit_bytes=40 * 2**20),
    )(
        *(
            pltpu.with_memory_space_constraint(operand, pltpu.VMEM)
            for operand in (arrived, table, spectra)
        ),
    )
    return (balanced.reshape(slots, 2, fields, modes, totals), balanced_grid)


def solution(mesh):
    placed = (P(None, "fld", "lat", None, None), P("lat", "fld", None, None), P(), P("fld"))
    return jax.shard_map(
        functools.partial(per_device, mesh.shape["lat"], mesh.shape["fld"]),
        mesh=mesh,
        in_specs=placed,
        out_specs=(P("lat", None, None, "fld", None), P(None, "fld", "lat", None, None)),
        check_vma=False,
    )
```

```python
import functools

import jax
import jax.numpy as jnp
from jax import lax
from jax.experimental import pallas as pl
from jax.experimental.pallas import tpu as pltpu
from jax.sharding import PartitionSpec as P

MESH = pl.DeviceIdType.MESH

COS_SERIES = (
    0.9999992251396179,
    -19.738981246948242,
    64.92865753173828,
    -85.27162170410156,
    58.79049301147461,
    -21.07110595703125,
)
SIN_SERIES = (
    6.283185005187988,
    -41.341590881347656,
    81.59994506835938,
    -76.61447143554688,
    41.3428840637207,
    -12.471243858337402,
)


def polynomial(series, argument):
    total = jnp.full_like(argument, series[-1])
    for coefficient in series[-2::-1]:
        total = total * argument + coefficient
    return total


def round_up(value, multiple):
    return -(-value // multiple) * multiple


def for_partners(me, ranks, act):
    bits = ranks.bit_length() - 1
    if ranks != 1 << bits:

        def around(step, carry):
            act(lax.rem(me + step, ranks))
            return carry

        lax.fori_loop(1, ranks, around, 0)
        return
    flips = [(1 - 2 * ((me // (1 << bit)) % 2)) * (1 << bit) for bit in range(bits)]
    if ranks <= 16:
        for step in range(ranks - 1, 0, -1):
            act(me + sum(flips[bit] for bit in range(bits) if step >> bit & 1))
        return

    def across(index, carry):
        step = ranks - 1 - index
        act(me + sum(flips[bit] * ((step // (1 << bit)) % 2) for bit in range(bits)))
        return carry

    lax.fori_loop(0, ranks - 1, across, 0)


def kernel(
    sizes,
    grid_hbm,
    basis_ref,
    owner_hbm,
    speed_hbm,
    spectra_ref,
    arrived_ref,
    table,
    grid_ref,
    lines,
    basis,
    forward_out,
    forward_in,
    backward_out,
    backward_in,
    by_round,
    outgoing,
    owner_ref,
    speed_ref,
    own_sem,
    local_sems,
    basis_sems,
    forward_sems,
    backward_sems,
):
    (ranks, halves, slots, rounds, padded_rounds, fields, modes, pairs, wave_count) = sizes
    inner = fields * modes
    half_count = ranks * pairs
    columns = table.shape[2] // 2
    totals = basis.shape[2]
    me = lax.axis_index("lat")
    hemisphere = lax.axis_index("fld")
    other = halves - 1 - hemisphere

    barrier = pltpu.get_barrier_semaphore()

    for_partners(
        me,
        ranks,
        lambda peer: pl.semaphore_signal(
            barrier, inc=1, device_id=(peer, hemisphere), device_id_type=MESH
        ),
    )
    pl.semaphore_signal(barrier, inc=1, device_id=(me, other), device_id_type=MESH)

    own_side = basis.at[
        :, pl.ds(pl.multiple_of(hemisphere * half_count, half_count), half_count)
    ]
    own_copy = pltpu.make_async_copy(
        basis_ref.at[pl.ds(0, rounds), 0], own_side, own_sem
    )
    owner_copy = pltpu.make_async_copy(owner_hbm, owner_ref, local_sems.at[0])
    speed_copy = pltpu.make_async_copy(speed_hbm, speed_ref, local_sems.at[1])
    grid_copy = pltpu.make_async_copy(grid_hbm, grid_ref, local_sems.at[2])
    owner_copy.start()
    grid_copy.start()
    speed_copy.start()
    own_copy.start()

    together = max(1, 16 // padded_rounds)
    chunk = together * padded_rounds
    row_index = lax.broadcasted_iota(jnp.int32, (chunk, columns), 0)
    column = lax.broadcasted_iota(jnp.int32, (chunk, columns), 1)
    column_f = column.astype(jnp.float32)

    def fill(step, carry):
        wave = jnp.full((chunk, columns), -1, jnp.int32)
        for part in range(together):
            for index in range(rounds):
                number = owner_ref[(step * together + part) * slots + index]
                wave = jnp.where(row_index == part * padded_rounds + index, number, wave)
        product = wave.astype(jnp.float32) * column_f
        for pair in range(pairs):
            points = 20 + 4 * (me * pairs + pair)
            highest = jnp.minimum(wave_count - 1, (points - 1) // 2)
            points_f = jnp.full((1, columns), points, jnp.int32).astype(jnp.float32)
            inverse = 1.0 / points_f
            scaling = lax.rsqrt(points_f)
            turns = jnp.floor(product * inverse + 0.5)
            angle = (product - turns * points_f) * inverse
            square = angle * angle
            inside = (column < points) & (wave <= highest) & (wave >= 0)
            scale = jnp.where(inside, scaling, 0.0)
            cosine = polynomial(COS_SERIES, square) * scale
            sine = polynomial(SIN_SERIES, square) * (angle * scale)
            where = pl.ds(pl.multiple_of(step * chunk, chunk), chunk)
            table[pair, where, 0:columns] = cosine.astype(jnp.bfloat16)
            table[pair, where, columns : 2 * columns] = (-sine).astype(jnp.bfloat16)
        return carry

    owner_copy.wait()
    lax.fori_loop(0, ranks // together, fill, 0, unroll=2)

    grid_copy.wait()
    loaded = grid_ref[...].astype(jnp.float32).reshape(lines.shape[1], -1)
    for tile in range(columns // 128):
        lines[tile] = loaded[:, tile * 128 : (tile + 1) * 128]
    blocks = []
    width = halves * inner
    for pair in range(pairs):
        values = jnp.concatenate(
            [
                jnp.concatenate(
                    [
                        lines[tile, pl.ds(pair * halves + side, inner, stride=pairs * halves), :]
                        for tile in range(columns // 128)
                    ],
                    axis=1,
                )
                for side in range(halves)
            ],
            axis=0,
        ).astype(jnp.bfloat16)
        empty = jnp.zeros_like(values)
        both = jnp.concatenate(
            [
                jnp.concatenate([values, empty], axis=1),
                jnp.concatenate([empty, values], axis=1),
            ],
            axis=0,
        )
        found = lax.dot_general(
            table[pair], both, (((1,), (1,)), ((), ())), preferred_element_type=jnp.float32
        )
        blocks.append(found.reshape(ranks, padded_rounds, 2 * width))
    forward_out[:, :, 0 : 2 * width] = jnp.concatenate(blocks, axis=1).astype(jnp.bfloat16)

    pl.semaphore_wait(barrier, ranks)

    def send(out, into, sems):
        def one(peer):
            pltpu.make_async_remote_copy(
                src_ref=out.at[peer],
                dst_ref=into.at[me],
                send_sem=sems.at[0],
                recv_sem=sems.at[1],
                device_id=(peer, hemisphere),
                device_id_type=MESH,
            ).start()

        for_partners(me, ranks, one)
        into[me] = out[me]

    def wait(ref, sem):
        part = ref.at[pl.ds(0, ranks - 1)]
        pltpu.make_async_copy(part, part, sem).wait()

    send(forward_out, forward_in, forward_sems)
    basis_copy = pltpu.make_async_remote_copy(
        src_ref=basis_ref.at[pl.ds(0, rounds), 0],
        dst_ref=own_side,
        send_sem=basis_sems.at[0],
        recv_sem=basis_sems.at[1],
        device_id=(me, other),
        device_id_type=MESH,
    )
    basis_copy.start()

    speed_copy.wait()
    mode_index = lax.broadcasted_iota(jnp.int32, (modes, totals), 0)
    degree_i = lax.broadcasted_iota(jnp.int32, (modes, totals), 1)
    degree = degree_i.astype(jnp.float32)
    speeds = jnp.zeros((modes, totals), jnp.float32)
    for mode in range(modes):
        speeds = jnp.where(mode_index == mode, speed_ref[mode], speeds)
    stiffness = degree * (degree + 1.0) * speeds
    retained = 1.0 / (1.0 + stiffness)
    root_term = jnp.sqrt(stiffness)
    removed = stiffness * retained

    numbers = [owner_ref[me * slots + index] for index in range(rounds)]
    outgoing[...] = jnp.zeros_like(outgoing)

    wait(forward_in, forward_sems.at[1])
    by_round[...] = forward_in[...].astype(jnp.float32).reshape(by_round.shape)
    own_copy.wait()
    basis_copy.wait_recv()

    incoming = [
        by_round[pl.ds(index, half_count, stride=padded_rounds), :] for index in range(rounds)
    ]
    turned = [rows.T for rows in incoming]
    coefficients = [
        jnp.concatenate(
            [
                jnp.concatenate(
                    [
                        rows[part * width + side * inner : part * width + (side + 1) * inner]
                        for part in range(2)
                    ],
                    axis=0,
                )
                for side in range(halves)
            ],
            axis=1,
        ).astype(jnp.bfloat16)
        for rows in turned
    ]
    spectra = [
        jnp.dot(rows, basis[index], preferred_element_type=jnp.float32)
        for index, rows in enumerate(coefficients)
    ]
    balanced = []
    for index, rows in enumerate(spectra):
        kept = degree_i >= numbers[index]
        pieces = []
        for part in range(2):
            first = part * inner
            vorticity = rows[first : first + modes]
            divergence = rows[first + modes : first + 2 * modes]
            geopotential = rows[first + 2 * modes : first + 3 * modes]
            rossby_part = (root_term * vorticity - geopotential) * retained
            for value in (
                retained * vorticity + removed * root_term * rossby_part,
                retained * divergence,
                retained * geopotential - removed * rossby_part,
            ):
                pieces.append(jnp.where(kept, value, 0.0))
        balanced.append(jnp.concatenate(pieces, axis=0).astype(jnp.bfloat16))
    returned = [
        lax.dot_general(
            rows, basis[index], (((1,), (1,)), ((), ())), preferred_element_type=jnp.float32
        )
        for index, rows in enumerate(balanced)
    ]
    spare = by_round.shape[1] - 2 * width
    for index, rows in enumerate(returned):
        ordered = [
            rows[part * inner : (part + 1) * inner, side * half_count : (side + 1) * half_count]
            for part in range(2)
            for side in range(halves)
        ]
        if spare:
            ordered.append(jnp.zeros((spare, half_count), jnp.float32))
        weight = jnp.where(numbers[index] == 0, 1.0, 2.0)
        outgoing[pl.ds(index, half_count, stride=padded_rounds), :] = (
            jnp.concatenate(ordered, axis=0).T * weight
        )

    backward_out[...] = outgoing[...].astype(jnp.bfloat16).reshape(backward_out.shape)
    send(backward_out, backward_in, backward_sems)
    for index, rows in enumerate(balanced):
        spectra_ref[index] = rows
    wait(backward_in, backward_sems.at[1])

    arrived_ref[...] = backward_in[...]

    basis_copy.wait_send()
    wait(forward_out, forward_sems.at[0])
    wait(backward_out, backward_sems.at[0])


def finish(
    sizes,
    arrived_ref,
    table,
    spectra_ref,
    balanced_hbm,
    grid_hbm,
    zeros,
    lines,
    grid_ref,
    copy_sems,
):
    ranks, halves, slots, rounds, padded_rounds, inner, pairs = sizes
    columns = table.shape[2] // 2
    width = halves * inner
    copies = [
        pltpu.make_async_copy(
            spectra_ref, balanced_hbm.at[pl.ds(0, rounds)], copy_sems.at[0]
        )
    ]
    copies[0].start()
    if rounds < slots:
        zeros[...] = jnp.zeros_like(zeros)
    for start in range(rounds, slots, rounds):
        count = min(rounds, slots - start)
        copies.append(
            pltpu.make_async_copy(
                zeros.at[pl.ds(0, count)],
                balanced_hbm.at[pl.ds(start, count)],
                copy_sems.at[len(copies)],
            )
        )
        copies[-1].start()

    for tile in range(columns // 128, lines.shape[0]):
        lines[tile] = jnp.zeros(lines.shape[1:], jnp.float32)
    for pair in range(pairs):
        first = pair * padded_rounds
        arrived = (
            arrived_ref[...]
            .astype(jnp.float32)[:, first : first + padded_rounds]
            .reshape(ranks * padded_rounds, arrived_ref.shape[2])
            .T
        )
        result = jnp.zeros((width, columns), jnp.float32)
        for part in range(2):
            result = result + jnp.dot(
                arrived[part * width : (part + 1) * width].astype(jnp.bfloat16),
                table[pair, :, part * columns : (part + 1) * columns],
                preferred_element_type=jnp.float32,
            )
        for side in range(halves):
            where = pl.ds(pair * halves + side, inner, stride=pairs * halves)
            for tile in range(columns // 128):
                lines[tile, where, :] = result[
                    side * inner : (side + 1) * inner, tile * 128 : (tile + 1) * 128
                ]
    joined = jnp.concatenate([lines[tile] for tile in range(lines.shape[0])], axis=1)
    grid_ref[...] = joined.reshape(grid_ref.shape).astype(jnp.bfloat16)
    copies.append(pltpu.make_async_copy(grid_ref, grid_hbm, copy_sems.at[len(copies)]))
    copies[-1].start()
    for one in copies:
        one.wait()


def per_device(ranks, halves, grid_fields, legendre_basis, owner_list, wave_speed):
    fields, modes, pairs, hemis, padded = grid_fields.shape
    slots, _, half_count, totals = legendre_basis.shape
    wave_count = owner_list.shape[0]
    longest = 20 + 4 * (half_count - 1)
    highest = min(wave_count - 1, (longest - 1) // 2)
    rounds = min(slots, highest // ranks + 1)
    padded_rounds = round_up(rounds, 8)
    columns = min(padded, round_up(longest, 128))
    lanes = round_up(2 * hemis * fields * modes, 128)
    block_rows = pairs * padded_rounds
    sizes = (ranks, halves, slots, rounds, padded_rounds, fields, modes, pairs, wave_count)
    table_shape = (pairs, ranks * padded_rounds, 2 * columns)
    block = pltpu.VMEM((ranks, block_rows, lanes), jnp.bfloat16)
    line_scratch = [
        pltpu.VMEM(grid_fields.shape, jnp.bfloat16),
        pltpu.VMEM((padded // 128, fields * modes * pairs * hemis, 128), jnp.float32),
    ]
    spectra_shape = (rounds, 2 * fields * modes, totals)
    spectra, arrived, table = pl.pallas_call(
        functools.partial(kernel, sizes),
        out_shape=(
            pltpu.VMEM(spectra_shape, jnp.bfloat16),
            block,
            pltpu.VMEM(table_shape, jnp.bfloat16),
        ),
        in_specs=[pl.BlockSpec(memory_space=pltpu.HBM)] * 4,
        out_specs=[pl.BlockSpec(memory_space=pltpu.VMEM)] * 3,
        scratch_shapes=line_scratch
        + [
            pltpu.VMEM((rounds, hemis * half_count, totals), jnp.bfloat16),
            block,
            block,
            block,
            block,
            pltpu.VMEM((ranks * block_rows, lanes), jnp.float32),
            pltpu.VMEM((ranks * block_rows, lanes), jnp.float32),
            pltpu.SMEM(owner_list.shape, jnp.int32),
            pltpu.SMEM(wave_speed.shape, jnp.float32),
            pltpu.SemaphoreType.DMA,
            pltpu.SemaphoreType.DMA((3,)),
            pltpu.SemaphoreType.DMA((2,)),
            pltpu.SemaphoreType.DMA((2,)),
            pltpu.SemaphoreType.DMA((2,)),
        ],
        compiler_params=pltpu.CompilerParams(
            collective_id=0, has_side_effects=True, vmem_limit_bytes=40 * 2**20
        ),
    )(
        *(
            pltpu.with_memory_space_constraint(operand, pltpu.HBM)
            for operand in (grid_fields, legendre_basis, owner_list, wave_speed)
        ),
    )
    copies = 2 + -(-(slots - rounds) // rounds)
    balanced, balanced_grid = pl.pallas_call(
        functools.partial(
            finish, (ranks, halves, slots, rounds, padded_rounds, fields * modes, pairs)
        ),
        out_shape=(
            pltpu.HBM((slots,) + spectra_shape[1:], jnp.bfloat16),
            pltpu.HBM(grid_fields.shape, jnp.bfloat16),
        ),
        in_specs=[pl.BlockSpec(memory_space=pltpu.VMEM)] * 3,
        out_specs=[pl.BlockSpec(memory_space=pltpu.HBM)] * 2,
        scratch_shapes=[pltpu.VMEM(spectra_shape, jnp.bfloat16)]
        + line_scratch[::-1]
        + [pltpu.SemaphoreType.DMA((copies,))],
        compiler_params=pltpu.CompilerParams(vmem_limit_bytes=40 * 2**20),
    )(
        *(
            pltpu.with_memory_space_constraint(operand, pltpu.VMEM)
            for operand in (arrived, table, spectra)
        ),
    )
    return (balanced.reshape(slots, 2, fields, modes, totals), balanced_grid)


def solution(mesh):
    placed = (P(None, "fld", "lat", None, None), P("lat", "fld", None, None), P(), P("fld"))
    return jax.shard_map(
        functools.partial(per_device, mesh.shape["lat"], mesh.shape["fld"]),
        mesh=mesh,
        in_specs=placed,
        out_specs=(P("lat", None, None, "fld", None), P(None, "fld", "lat", None, None)),
        check_vma=False,
    )
```

```python
import functools

import jax
import jax.numpy as jnp
from jax import lax
from jax.experimental import pallas as pl
from jax.experimental.pallas import tpu as pltpu
from jax.sharding import PartitionSpec as P

MESH = pl.DeviceIdType.MESH

COS_SERIES = (
    0.9999992251396179,
    -19.738981246948242,
    64.92865753173828,
    -85.27162170410156,
    58.79049301147461,
    -21.07110595703125,
)
SIN_SERIES = (
    6.283185005187988,
    -41.341590881347656,
    81.59994506835938,
    -76.61447143554688,
    41.3428840637207,
    -12.471243858337402,
)


def polynomial(series, argument):
    total = jnp.full_like(argument, series[-1])
    for coefficient in series[-2::-1]:
        total = total * argument + coefficient
    return total


def round_up(value, multiple):
    return -(-value // multiple) * multiple


def for_partners(me, ranks, act):
    bits = ranks.bit_length() - 1
    if ranks != 1 << bits:

        def around(step, carry):
            act(lax.rem(me + step, ranks))
            return carry

        lax.fori_loop(1, ranks, around, 0)
        return
    flips = [(1 - 2 * ((me // (1 << bit)) % 2)) * (1 << bit) for bit in range(bits)]
    if ranks <= 16:
        for step in range(ranks - 1, 0, -1):
            act(me + sum(flips[bit] for bit in range(bits) if step >> bit & 1))
        return

    def across(index, carry):
        step = ranks - 1 - index
        act(me + sum(flips[bit] * ((step // (1 << bit)) % 2) for bit in range(bits)))
        return carry

    lax.fori_loop(0, ranks - 1, across, 0)


def kernel(
    sizes,
    grid_hbm,
    basis_ref,
    owner_hbm,
    speed_hbm,
    spectra_ref,
    arrived_ref,
    table,
    grid_ref,
    lines,
    basis,
    forward_out,
    forward_in,
    backward_out,
    backward_in,
    by_round,
    outgoing,
    owner_ref,
    speed_ref,
    own_sem,
    local_sems,
    basis_sems,
    forward_sems,
    backward_sems,
):
    (ranks, halves, slots, rounds, padded_rounds, fields, modes, pairs, wave_count) = sizes
    inner = fields * modes
    half_count = ranks * pairs
    columns = table.shape[2] // 2
    totals = basis.shape[2]
    me = lax.axis_index("lat")
    hemisphere = lax.axis_index("fld")
    other = halves - 1 - hemisphere

    barrier = pltpu.get_barrier_semaphore()

    for_partners(
        me,
        ranks,
        lambda peer: pl.semaphore_signal(
            barrier, inc=1, device_id=(peer, hemisphere), device_id_type=MESH
        ),
    )
    pl.semaphore_signal(barrier, inc=1, device_id=(me, other), device_id_type=MESH)

    own_side = basis.at[
        :, pl.ds(pl.multiple_of(hemisphere * half_count, half_count), half_count)
    ]
    own_copy = pltpu.make_async_copy(
        basis_ref.at[pl.ds(0, rounds), 0], own_side, own_sem
    )
    owner_copy = pltpu.make_async_copy(owner_hbm, owner_ref, local_sems.at[0])
    speed_copy = pltpu.make_async_copy(speed_hbm, speed_ref, local_sems.at[1])
    grid_copy = pltpu.make_async_copy(grid_hbm, grid_ref, local_sems.at[2])
    owner_copy.start()
    grid_copy.start()
    speed_copy.start()
    own_copy.start()

    together = max(1, 16 // padded_rounds)
    chunk = together * padded_rounds
    row_index = lax.broadcasted_iota(jnp.int32, (chunk, columns), 0)
    column = lax.broadcasted_iota(jnp.int32, (chunk, columns), 1)
    column_f = column.astype(jnp.float32)

    def fill(step, carry):
        wave = jnp.full((chunk, columns), -1, jnp.int32)
        for part in range(together):
            for index in range(rounds):
                number = owner_ref[(step * together + part) * slots + index]
                wave = jnp.where(row_index == part * padded_rounds + index, number, wave)
        product = wave.astype(jnp.float32) * column_f
        for pair in range(pairs):
            points = 20 + 4 * (me * pairs + pair)
            highest = jnp.minimum(wave_count - 1, (points - 1) // 2)
            points_f = jnp.full((1, columns), points, jnp.int32).astype(jnp.float32)
            inverse = 1.0 / points_f
            scaling = lax.rsqrt(points_f)
            turns = jnp.floor(product * inverse + 0.5)
            angle = (product - turns * points_f) * inverse
            square = angle * angle
            inside = (column < points) & (wave <= highest) & (wave >= 0)
            scale = jnp.where(inside, scaling, 0.0)
            cosine = polynomial(COS_SERIES, square) * scale
            sine = polynomial(SIN_SERIES, square) * (angle * scale)
            where = pl.ds(pl.multiple_of(step * chunk, chunk), chunk)
            table[pair, where, 0:columns] = cosine.astype(jnp.bfloat16)
            table[pair, where, columns : 2 * columns] = (-sine).astype(jnp.bfloat16)
        return carry

    owner_copy.wait()
    lax.fori_loop(0, ranks // together, fill, 0, unroll=2)

    grid_copy.wait()
    loaded = grid_ref[...].astype(jnp.float32).reshape(lines.shape[1], -1)
    for tile in range(columns // 128):
        lines[tile] = loaded[:, tile * 128 : (tile + 1) * 128]
    blocks = []
    width = halves * inner
    for pair in range(pairs):
        values = jnp.concatenate(
            [
                jnp.concatenate(
                    [
                        lines[tile, pl.ds(pair * halves + side, inner, stride=pairs * halves), :]
                        for tile in range(columns // 128)
                    ],
                    axis=1,
                )
                for side in range(halves)
            ],
            axis=0,
        ).astype(jnp.bfloat16)
        empty = jnp.zeros_like(values)
        both = jnp.concatenate(
            [
                jnp.concatenate([values, empty], axis=1),
                jnp.concatenate([empty, values], axis=1),
            ],
            axis=0,
        )
        found = lax.dot_general(
            table[pair], both, (((1,), (1,)), ((), ())), preferred_element_type=jnp.float32
        )
        blocks.append(found.reshape(ranks, padded_rounds, 2 * width))
    forward_out[:, :, 0 : 2 * width] = jnp.concatenate(blocks, axis=1).astype(jnp.bfloat16)

    pl.semaphore_wait(barrier, ranks)

    def send(out, into, sems):
        def one(peer):
            pltpu.make_async_remote_copy(
                src_ref=out.at[peer],
                dst_ref=into.at[me],
                send_sem=sems.at[0],
                recv_sem=sems.at[1],
                device_id=(peer, hemisphere),
                device_id_type=MESH,
            ).start()

        for_partners(me, ranks, one)
        into[me] = out[me]

    def wait(ref, sem):
        part = ref.at[pl.ds(0, ranks - 1)]
        pltpu.make_async_copy(part, part, sem).wait()

    own_copy.wait()
    basis_copy = pltpu.make_async_remote_copy(
        src_ref=own_side,
        dst_ref=own_side,
        send_sem=basis_sems.at[0],
        recv_sem=basis_sems.at[1],
        device_id=(me, other),
        device_id_type=MESH,
    )
    basis_copy.start()
    send(forward_out, forward_in, forward_sems)

    speed_copy.wait()
    mode_index = lax.broadcasted_iota(jnp.int32, (modes, totals), 0)
    degree_i = lax.broadcasted_iota(jnp.int32, (modes, totals), 1)
    degree = degree_i.astype(jnp.float32)
    speeds = jnp.zeros((modes, totals), jnp.float32)
    for mode in range(modes):
        speeds = jnp.where(mode_index == mode, speed_ref[mode], speeds)
    stiffness = degree * (degree + 1.0) * speeds
    retained = 1.0 / (1.0 + stiffness)
    root_term = jnp.sqrt(stiffness)
    removed = stiffness * retained

    numbers = [owner_ref[me * slots + index] for index in range(rounds)]
    outgoing[...] = jnp.zeros_like(outgoing)

    wait(forward_in, forward_sems.at[1])
    by_round[...] = forward_in[...].astype(jnp.float32).reshape(by_round.shape)
    basis_copy.wait_recv()

    incoming = [
        by_round[pl.ds(index, half_count, stride=padded_rounds), :] for index in range(rounds)
    ]
    turned = [rows.T for rows in incoming]
    coefficients = [
        jnp.concatenate(
            [
                jnp.concatenate(
                    [
                        rows[part * width + side * inner : part * width + (side + 1) * inner]
                        for part in range(2)
                    ],
                    axis=0,
                )
                for side in range(halves)
            ],
            axis=1,
        ).astype(jnp.bfloat16)
        for rows in turned
    ]
    spectra = [
        jnp.dot(rows, basis[index], preferred_element_type=jnp.float32)
        for index, rows in enumerate(coefficients)
    ]
    balanced = []
    for index, rows in enumerate(spectra):
        kept = degree_i >= numbers[index]
        pieces = []
        for part in range(2):
            first = part * inner
            vorticity = rows[first : first + modes]
            divergence = rows[first + modes : first + 2 * modes]
            geopotential = rows[first + 2 * modes : first + 3 * modes]
            rossby_part = (root_term * vorticity - geopotential) * retained
            for value in (
                retained * vorticity + removed * root_term * rossby_part,
                retained * divergence,
                retained * geopotential - removed * rossby_part,
            ):
                pieces.append(jnp.where(kept, value, 0.0))
        balanced.append(jnp.concatenate(pieces, axis=0).astype(jnp.bfloat16))
    returned = [
        lax.dot_general(
            rows, basis[index], (((1,), (1,)), ((), ())), preferred_element_type=jnp.float32
        )
        for index, rows in enumerate(balanced)
    ]
    spare = by_round.shape[1] - 2 * width
    for index, rows in enumerate(returned):
        ordered = [
            rows[part * inner : (part + 1) * inner, side * half_count : (side + 1) * half_count]
            for part in range(2)
            for side in range(halves)
        ]
        if spare:
            ordered.append(jnp.zeros((spare, half_count), jnp.float32))
        weight = jnp.where(numbers[index] == 0, 1.0, 2.0)
        outgoing[pl.ds(index, half_count, stride=padded_rounds), :] = (
            jnp.concatenate(ordered, axis=0).T * weight
        )

    backward_out[...] = outgoing[...].astype(jnp.bfloat16).reshape(backward_out.shape)
    send(backward_out, backward_in, backward_sems)
    for index, rows in enumerate(balanced):
        spectra_ref[index] = rows
    wait(backward_in, backward_sems.at[1])

    arrived_ref[...] = backward_in[...]

    basis_copy.wait_send()
    wait(forward_out, forward_sems.at[0])
    wait(backward_out, backward_sems.at[0])


def finish(
    sizes,
    arrived_ref,
    table,
    spectra_ref,
    balanced_hbm,
    grid_hbm,
    zeros,
    lines,
    grid_ref,
    copy_sems,
):
    ranks, halves, slots, rounds, padded_rounds, inner, pairs = sizes
    columns = table.shape[2] // 2
    width = halves * inner
    copies = [
        pltpu.make_async_copy(
            spectra_ref, balanced_hbm.at[pl.ds(0, rounds)], copy_sems.at[0]
        )
    ]
    copies[0].start()
    if rounds < slots:
        zeros[...] = jnp.zeros_like(zeros)
    for start in range(rounds, slots, rounds):
        count = min(rounds, slots - start)
        copies.append(
            pltpu.make_async_copy(
                zeros.at[pl.ds(0, count)],
                balanced_hbm.at[pl.ds(start, count)],
                copy_sems.at[len(copies)],
            )
        )
        copies[-1].start()

    for tile in range(columns // 128, lines.shape[0]):
        lines[tile] = jnp.zeros(lines.shape[1:], jnp.float32)
    for pair in range(pairs):
        first = pair * padded_rounds
        arrived = (
            arrived_ref[...]
            .astype(jnp.float32)[:, first : first + padded_rounds]
            .reshape(ranks * padded_rounds, arrived_ref.shape[2])
            .T
        )
        result = jnp.zeros((width, columns), jnp.float32)
        for part in range(2):
            result = result + jnp.dot(
                arrived[part * width : (part + 1) * width].astype(jnp.bfloat16),
                table[pair, :, part * columns : (part + 1) * columns],
                preferred_element_type=jnp.float32,
            )
        for side in range(halves):
            where = pl.ds(pair * halves + side, inner, stride=pairs * halves)
            for tile in range(columns // 128):
                lines[tile, where, :] = result[
                    side * inner : (side + 1) * inner, tile * 128 : (tile + 1) * 128
                ]
    joined = jnp.concatenate([lines[tile] for tile in range(lines.shape[0])], axis=1)
    grid_ref[...] = joined.reshape(grid_ref.shape).astype(jnp.bfloat16)
    copies.append(pltpu.make_async_copy(grid_ref, grid_hbm, copy_sems.at[len(copies)]))
    copies[-1].start()
    for one in copies:
        one.wait()


def per_device(ranks, halves, grid_fields, legendre_basis, owner_list, wave_speed):
    fields, modes, pairs, hemis, padded = grid_fields.shape
    slots, _, half_count, totals = legendre_basis.shape
    wave_count = owner_list.shape[0]
    longest = 20 + 4 * (half_count - 1)
    highest = min(wave_count - 1, (longest - 1) // 2)
    rounds = min(slots, highest // ranks + 1)
    padded_rounds = round_up(rounds, 8)
    columns = min(padded, round_up(longest, 128))
    lanes = round_up(2 * hemis * fields * modes, 128)
    block_rows = pairs * padded_rounds
    sizes = (ranks, halves, slots, rounds, padded_rounds, fields, modes, pairs, wave_count)
    table_shape = (pairs, ranks * padded_rounds, 2 * columns)
    block = pltpu.VMEM((ranks, block_rows, lanes), jnp.bfloat16)
    line_scratch = [
        pltpu.VMEM(grid_fields.shape, jnp.bfloat16),
        pltpu.VMEM((padded // 128, fields * modes * pairs * hemis, 128), jnp.float32),
    ]
    spectra_shape = (rounds, 2 * fields * modes, totals)
    spectra, arrived, table = pl.pallas_call(
        functools.partial(kernel, sizes),
        out_shape=(
            pltpu.VMEM(spectra_shape, jnp.bfloat16),
            block,
            pltpu.VMEM(table_shape, jnp.bfloat16),
        ),
        in_specs=[pl.BlockSpec(memory_space=pltpu.HBM)] * 4,
        out_specs=[pl.BlockSpec(memory_space=pltpu.VMEM)] * 3,
        scratch_shapes=line_scratch
        + [
            pltpu.VMEM((rounds, hemis * half_count, totals), jnp.bfloat16),
            block,
            block,
            block,
            block,
            pltpu.VMEM((ranks * block_rows, lanes), jnp.float32),
            pltpu.VMEM((ranks * block_rows, lanes), jnp.float32),
            pltpu.SMEM(owner_list.shape, jnp.int32),
            pltpu.SMEM(wave_speed.shape, jnp.float32),
            pltpu.SemaphoreType.DMA,
            pltpu.SemaphoreType.DMA((3,)),
            pltpu.SemaphoreType.DMA((2,)),
            pltpu.SemaphoreType.DMA((2,)),
            pltpu.SemaphoreType.DMA((2,)),
        ],
        compiler_params=pltpu.CompilerParams(
            collective_id=0, has_side_effects=True, vmem_limit_bytes=40 * 2**20
        ),
    )(
        *(
            pltpu.with_memory_space_constraint(operand, pltpu.HBM)
            for operand in (grid_fields, legendre_basis, owner_list, wave_speed)
        ),
    )
    copies = 2 + -(-(slots - rounds) // rounds)
    balanced, balanced_grid = pl.pallas_call(
        functools.partial(
            finish, (ranks, halves, slots, rounds, padded_rounds, fields * modes, pairs)
        ),
        out_shape=(
            pltpu.HBM((slots,) + spectra_shape[1:], jnp.bfloat16),
            pltpu.HBM(grid_fields.shape, jnp.bfloat16),
        ),
        in_specs=[pl.BlockSpec(memory_space=pltpu.VMEM)] * 3,
        out_specs=[pl.BlockSpec(memory_space=pltpu.HBM)] * 2,
        scratch_shapes=[pltpu.VMEM(spectra_shape, jnp.bfloat16)]
        + line_scratch[::-1]
        + [pltpu.SemaphoreType.DMA((copies,))],
        compiler_params=pltpu.CompilerParams(vmem_limit_bytes=40 * 2**20),
    )(
        *(
            pltpu.with_memory_space_constraint(operand, pltpu.VMEM)
            for operand in (arrived, table, spectra)
        ),
    )
    return (balanced.reshape(slots, 2, fields, modes, totals), balanced_grid)


def solution(mesh):
    placed = (P(None, "fld", "lat", None, None), P("lat", "fld", None, None), P(), P("fld"))
    return jax.shard_map(
        functools.partial(per_device, mesh.shape["lat"], mesh.shape["fld"]),
        mesh=mesh,
        in_specs=placed,
        out_specs=(P("lat", None, None, "fld", None), P(None, "fld", "lat", None, None)),
        check_vma=False,
    )
```

```python
import functools

import jax
import jax.numpy as jnp
from jax import lax
from jax.experimental import pallas as pl
from jax.experimental.pallas import tpu as pltpu
from jax.sharding import PartitionSpec as P

MESH = pl.DeviceIdType.MESH

COS_SERIES = (
    0.9999992251396179,
    -19.738981246948242,
    64.92865753173828,
    -85.27162170410156,
    58.79049301147461,
    -21.07110595703125,
)
SIN_SERIES = (
    6.283185005187988,
    -41.341590881347656,
    81.59994506835938,
    -76.61447143554688,
    41.3428840637207,
    -12.471243858337402,
)


def polynomial(series, argument):
    total = jnp.full_like(argument, series[-1])
    for coefficient in series[-2::-1]:
        total = total * argument + coefficient
    return total


def round_up(value, multiple):
    return -(-value // multiple) * multiple


def for_partners(me, ranks, act):
    bits = ranks.bit_length() - 1
    if ranks != 1 << bits:

        def around(step, carry):
            act(lax.rem(me + step, ranks))
            return carry

        lax.fori_loop(1, ranks, around, 0)
        return
    flips = [(1 - 2 * ((me // (1 << bit)) % 2)) * (1 << bit) for bit in range(bits)]
    if ranks <= 16:
        for step in range(ranks - 1, 0, -1):
            act(me + sum(flips[bit] for bit in range(bits) if step >> bit & 1))
        return

    def across(index, carry):
        step = ranks - 1 - index
        act(me + sum(flips[bit] * ((step // (1 << bit)) % 2) for bit in range(bits)))
        return carry

    lax.fori_loop(0, ranks - 1, across, 0)


def kernel(
    sizes,
    grid_hbm,
    basis_ref,
    owner_hbm,
    speed_hbm,
    spectra_ref,
    arrived_ref,
    table,
    grid_ref,
    lines,
    basis,
    forward_out,
    forward_in,
    backward_out,
    backward_in,
    by_round,
    outgoing,
    owner_ref,
    speed_ref,
    own_sem,
    local_sems,
    basis_sems,
    forward_sems,
    backward_sems,
):
    (ranks, halves, slots, rounds, padded_rounds, fields, modes, pairs, wave_count) = sizes
    inner = fields * modes
    half_count = ranks * pairs
    columns = table.shape[2] // 2
    totals = basis.shape[2]
    me = lax.axis_index("lat")
    hemisphere = lax.axis_index("fld")
    other = halves - 1 - hemisphere

    barrier = pltpu.get_barrier_semaphore()

    for_partners(
        me,
        ranks,
        lambda peer: pl.semaphore_signal(
            barrier, inc=1, device_id=(peer, hemisphere), device_id_type=MESH
        ),
    )
    pl.semaphore_signal(barrier, inc=1, device_id=(me, other), device_id_type=MESH)

    own_side = basis.at[
        :, pl.ds(pl.multiple_of(hemisphere * half_count, half_count), half_count)
    ]
    own_copy = pltpu.make_async_copy(
        basis_ref.at[pl.ds(0, rounds), 0], own_side, own_sem
    )
    owner_copy = pltpu.make_async_copy(owner_hbm, owner_ref, local_sems.at[0])
    speed_copy = pltpu.make_async_copy(speed_hbm, speed_ref, local_sems.at[1])
    grid_copy = pltpu.make_async_copy(grid_hbm, grid_ref, local_sems.at[2])
    owner_copy.start()
    grid_copy.start()
    speed_copy.start()
    own_copy.start()

    together = max(1, 16 // padded_rounds)
    chunk = together * padded_rounds
    row_index = lax.broadcasted_iota(jnp.int32, (chunk, 128), 0)
    column = lax.broadcasted_iota(jnp.int32, (chunk, columns), 1)
    column_f = column.astype(jnp.float32)

    def fill(step, carry):
        wave = jnp.full((chunk, 128), -1, jnp.int32)
        for part in range(together):
            for index in range(rounds):
                number = owner_ref[(step * together + part) * slots + index]
                wave = jnp.where(row_index == part * padded_rounds + index, number, wave)
        wave = jnp.concatenate([wave] * (columns // 128), axis=1)
        product = wave.astype(jnp.float32) * column_f
        for pair in range(pairs):
            points = 20 + 4 * (me * pairs + pair)
            highest = jnp.minimum(wave_count - 1, (points - 1) // 2)
            points_f = jnp.full((1, columns), points, jnp.int32).astype(jnp.float32)
            inverse = 1.0 / points_f
            scaling = lax.rsqrt(points_f)
            turns = jnp.floor(product * inverse + 0.5)
            angle = (product - turns * points_f) * inverse
            square = angle * angle
            inside = (column < points) & (wave <= highest) & (wave >= 0)
            scale = jnp.where(inside, scaling, 0.0)
            cosine = polynomial(COS_SERIES, square) * scale
            sine = polynomial(SIN_SERIES, square) * (angle * scale)
            where = pl.ds(pl.multiple_of(step * chunk, chunk), chunk)
            table[pair, where, 0:columns] = cosine.astype(jnp.bfloat16)
            table[pair, where, columns : 2 * columns] = (-sine).astype(jnp.bfloat16)
        return carry

    owner_copy.wait()
    lax.fori_loop(0, ranks // together, fill, 0, unroll=8 if ranks <= 16 else 1)

    grid_copy.wait()
    loaded = grid_ref[...].astype(jnp.float32).reshape(lines.shape[1], -1)
    for tile in range(columns // 128):
        lines[tile] = loaded[:, tile * 128 : (tile + 1) * 128]
    blocks = []
    width = halves * inner
    for pair in range(pairs):
        values = jnp.concatenate(
            [
                jnp.concatenate(
                    [
                        lines[tile, pl.ds(pair * halves + side, inner, stride=pairs * halves), :]
                        for tile in range(columns // 128)
                    ],
                    axis=1,
                )
                for side in range(halves)
            ],
            axis=0,
        ).astype(jnp.bfloat16)
        empty = jnp.zeros_like(values)
        both = jnp.concatenate(
            [
                jnp.concatenate([values, empty], axis=1),
                jnp.concatenate([empty, values], axis=1),
            ],
            axis=0,
        )
        found = lax.dot_general(
            table[pair], both, (((1,), (1,)), ((), ())), preferred_element_type=jnp.float32
        )
        blocks.append(found.reshape(ranks, padded_rounds, 2 * width))
    forward_out[:, :, 0 : 2 * width] = jnp.concatenate(blocks, axis=1).astype(jnp.bfloat16)

    pl.semaphore_wait(barrier, ranks)

    def send(out, into, sems):
        def one(peer):
            pltpu.make_async_remote_copy(
                src_ref=out.at[peer],
                dst_ref=into.at[me],
                send_sem=sems.at[0],
                recv_sem=sems.at[1],
                device_id=(peer, hemisphere),
                device_id_type=MESH,
            ).start()

        for_partners(me, ranks, one)
        into[me] = out[me]

    def wait(ref, sem):
        part = ref.at[pl.ds(0, ranks - 1)]
        pltpu.make_async_copy(part, part, sem).wait()

    own_copy.wait()
    basis_copy = pltpu.make_async_remote_copy(
        src_ref=own_side,
        dst_ref=own_side,
        send_sem=basis_sems.at[0],
        recv_sem=basis_sems.at[1],
        device_id=(me, other),
        device_id_type=MESH,
    )
    basis_copy.start()
    send(forward_out, forward_in, forward_sems)

    speed_copy.wait()
    mode_index = lax.broadcasted_iota(jnp.int32, (modes, totals), 0)
    degree_i = lax.broadcasted_iota(jnp.int32, (modes, totals), 1)
    degree = degree_i.astype(jnp.float32)
    speeds = jnp.zeros((modes, totals), jnp.float32)
    for mode in range(modes):
        speeds = jnp.where(mode_index == mode, speed_ref[mode], speeds)
    stiffness = degree * (degree + 1.0) * speeds
    retained = 1.0 / (1.0 + stiffness)
    root_term = jnp.sqrt(stiffness)
    removed = stiffness * retained

    numbers = [owner_ref[me * slots + index] for index in range(rounds)]
    outgoing[...] = jnp.zeros_like(outgoing)

    wait(forward_in, forward_sems.at[1])
    by_round[...] = forward_in[...].astype(jnp.float32).reshape(by_round.shape)
    basis_copy.wait_recv()

    incoming = [
        by_round[pl.ds(index, half_count, stride=padded_rounds), :] for index in range(rounds)
    ]
    turned = [rows.T for rows in incoming]
    coefficients = [
        jnp.concatenate(
            [
                jnp.concatenate(
                    [
                        rows[part * width + side * inner : part * width + (side + 1) * inner]
                        for part in range(2)
                    ],
                    axis=0,
                )
                for side in range(halves)
            ],
            axis=1,
        ).astype(jnp.bfloat16)
        for rows in turned
    ]
    spectra = [
        jnp.dot(rows, basis[index], preferred_element_type=jnp.float32)
        for index, rows in enumerate(coefficients)
    ]
    balanced = []
    for index, rows in enumerate(spectra):
        kept = degree_i >= numbers[index]
        pieces = []
        for part in range(2):
            first = part * inner
            vorticity = rows[first : first + modes]
            divergence = rows[first + modes : first + 2 * modes]
            geopotential = rows[first + 2 * modes : first + 3 * modes]
            rossby_part = (root_term * vorticity - geopotential) * retained
            for value in (
                retained * vorticity + removed * root_term * rossby_part,
                retained * divergence,
                retained * geopotential - removed * rossby_part,
            ):
                pieces.append(jnp.where(kept, value, 0.0))
        balanced.append(jnp.concatenate(pieces, axis=0).astype(jnp.bfloat16))
    returned = [
        lax.dot_general(
            rows, basis[index], (((1,), (1,)), ((), ())), preferred_element_type=jnp.float32
        )
        for index, rows in enumerate(balanced)
    ]
    spare = by_round.shape[1] - 2 * width
    for index, rows in enumerate(returned):
        ordered = [
            rows[part * inner : (part + 1) * inner, side * half_count : (side + 1) * half_count]
            for part in range(2)
            for side in range(halves)
        ]
        if spare:
            ordered.append(jnp.zeros((spare, half_count), jnp.float32))
        weight = jnp.where(numbers[index] == 0, 1.0, 2.0)
        outgoing[pl.ds(index, half_count, stride=padded_rounds), :] = (
            jnp.concatenate(ordered, axis=0).T * weight
        )

    backward_out[...] = outgoing[...].astype(jnp.bfloat16).reshape(backward_out.shape)
    send(backward_out, backward_in, backward_sems)
    for index, rows in enumerate(balanced):
        spectra_ref[index] = rows
    wait(backward_in, backward_sems.at[1])

    arrived_ref[...] = backward_in[...]

    basis_copy.wait_send()
    wait(forward_out, forward_sems.at[0])
    wait(backward_out, backward_sems.at[0])


def finish(
    sizes,
    arrived_ref,
    table,
    spectra_ref,
    balanced_hbm,
    grid_hbm,
    zeros,
    lines,
    grid_ref,
    copy_sems,
):
    ranks, halves, slots, rounds, padded_rounds, inner, pairs = sizes
    columns = table.shape[2] // 2
    width = halves * inner
    copies = [
        pltpu.make_async_copy(
            spectra_ref, balanced_hbm.at[pl.ds(0, rounds)], copy_sems.at[0]
        )
    ]
    copies[0].start()
    if rounds < slots:
        zeros[...] = jnp.zeros_like(zeros)
    for start in range(rounds, slots, rounds):
        count = min(rounds, slots - start)
        copies.append(
            pltpu.make_async_copy(
                zeros.at[pl.ds(0, count)],
                balanced_hbm.at[pl.ds(start, count)],
                copy_sems.at[len(copies)],
            )
        )
        copies[-1].start()

    for tile in range(columns // 128, lines.shape[0]):
        lines[tile] = jnp.zeros(lines.shape[1:], jnp.float32)
    for pair in range(pairs):
        first = pair * padded_rounds
        arrived = (
            arrived_ref[...]
            .astype(jnp.float32)[:, first : first + padded_rounds]
            .reshape(ranks * padded_rounds, arrived_ref.shape[2])
            .T
        )
        result = jnp.zeros((width, columns), jnp.float32)
        for part in range(2):
            result = result + jnp.dot(
                arrived[part * width : (part + 1) * width].astype(jnp.bfloat16),
                table[pair, :, part * columns : (part + 1) * columns],
                preferred_element_type=jnp.float32,
            )
        for side in range(halves):
            where = pl.ds(pair * halves + side, inner, stride=pairs * halves)
            for tile in range(columns // 128):
                lines[tile, where, :] = result[
                    side * inner : (side + 1) * inner, tile * 128 : (tile + 1) * 128
                ]
    joined = jnp.concatenate([lines[tile] for tile in range(lines.shape[0])], axis=1)
    grid_ref[...] = joined.reshape(grid_ref.shape).astype(jnp.bfloat16)
    copies.append(pltpu.make_async_copy(grid_ref, grid_hbm, copy_sems.at[len(copies)]))
    copies[-1].start()
    for one in copies:
        one.wait()


def per_device(ranks, halves, grid_fields, legendre_basis, owner_list, wave_speed):
    fields, modes, pairs, hemis, padded = grid_fields.shape
    slots, _, half_count, totals = legendre_basis.shape
    wave_count = owner_list.shape[0]
    longest = 20 + 4 * (half_count - 1)
    highest = min(wave_count - 1, (longest - 1) // 2)
    rounds = min(slots, highest // ranks + 1)
    padded_rounds = round_up(rounds, 8)
    columns = min(padded, round_up(longest, 128))
    lanes = round_up(2 * hemis * fields * modes, 128)
    block_rows = pairs * padded_rounds
    sizes = (ranks, halves, slots, rounds, padded_rounds, fields, modes, pairs, wave_count)
    table_shape = (pairs, ranks * padded_rounds, 2 * columns)
    block = pltpu.VMEM((ranks, block_rows, lanes), jnp.bfloat16)
    line_scratch = [
        pltpu.VMEM(grid_fields.shape, jnp.bfloat16),
        pltpu.VMEM((padded // 128, fields * modes * pairs * hemis, 128), jnp.float32),
    ]
    spectra_shape = (rounds, 2 * fields * modes, totals)
    spectra, arrived, table = pl.pallas_call(
        functools.partial(kernel, sizes),
        out_shape=(
            pltpu.VMEM(spectra_shape, jnp.bfloat16),
            block,
            pltpu.VMEM(table_shape, jnp.bfloat16),
        ),
        in_specs=[pl.BlockSpec(memory_space=pltpu.HBM)] * 4,
        out_specs=[pl.BlockSpec(memory_space=pltpu.VMEM)] * 3,
        scratch_shapes=line_scratch
        + [
            pltpu.VMEM((rounds, hemis * half_count, totals), jnp.bfloat16),
            block,
            block,
            block,
            block,
            pltpu.VMEM((ranks * block_rows, lanes), jnp.float32),
            pltpu.VMEM((ranks * block_rows, lanes), jnp.float32),
            pltpu.SMEM(owner_list.shape, jnp.int32),
            pltpu.SMEM(wave_speed.shape, jnp.float32),
            pltpu.SemaphoreType.DMA,
            pltpu.SemaphoreType.DMA((3,)),
            pltpu.SemaphoreType.DMA((2,)),
            pltpu.SemaphoreType.DMA((2,)),
            pltpu.SemaphoreType.DMA((2,)),
        ],
        compiler_params=pltpu.CompilerParams(
            collective_id=0, has_side_effects=True, vmem_limit_bytes=40 * 2**20
        ),
    )(
        *(
            pltpu.with_memory_space_constraint(operand, pltpu.HBM)
            for operand in (grid_fields, legendre_basis, owner_list, wave_speed)
        ),
    )
    copies = 2 + -(-(slots - rounds) // rounds)
    balanced, balanced_grid = pl.pallas_call(
        functools.partial(
            finish, (ranks, halves, slots, rounds, padded_rounds, fields * modes, pairs)
        ),
        out_shape=(
            pltpu.HBM((slots,) + spectra_shape[1:], jnp.bfloat16),
            pltpu.HBM(grid_fields.shape, jnp.bfloat16),
        ),
        in_specs=[pl.BlockSpec(memory_space=pltpu.VMEM)] * 3,
        out_specs=[pl.BlockSpec(memory_space=pltpu.HBM)] * 2,
        scratch_shapes=[pltpu.VMEM(spectra_shape, jnp.bfloat16)]
        + line_scratch[::-1]
        + [pltpu.SemaphoreType.DMA((copies,))],
        compiler_params=pltpu.CompilerParams(vmem_limit_bytes=40 * 2**20),
    )(
        *(
            pltpu.with_memory_space_constraint(operand, pltpu.VMEM)
            for operand in (arrived, table, spectra)
        ),
    )
    return (balanced.reshape(slots, 2, fields, modes, totals), balanced_grid)


def solution(mesh):
    placed = (P(None, "fld", "lat", None, None), P("lat", "fld", None, None), P(), P("fld"))
    return jax.shard_map(
        functools.partial(per_device, mesh.shape["lat"], mesh.shape["fld"]),
        mesh=mesh,
        in_specs=placed,
        out_specs=(P("lat", None, None, "fld", None), P(None, "fld", "lat", None, None)),
        check_vma=False,
    )
```
